256 devices in a mesh: ctx: 32 (over x, y, core), tp: 8 (over z).
Axes of the slice: x: 4, y: 4, z: 8, core: 2. Of those that a mesh axis runs over, the one named last changes fastest.
Arguments:
- queries: bfloat16 [8192, 4096], P('ctx', 'tp'), may hold values from -8 to 8
- key_rows: bfloat16 [8192, 4096], P('ctx', 'tp'), may hold values from -8 to 8
- value_rows: bfloat16 [8192, 4096], P('ctx', 'tp'), may hold values from -6 to 6
- log_decay: float32 [32, 8192], P('tp', 'ctx'), may hold values from -1 to 0, as said below
- write_rate: float32 [32, 8192], P('tp', 'ctx'), may hold values from 0 to 1, as said below
- gate_input: bfloat16 [8192, 4096], P('ctx', 'tp'), may hold values from -6 to 6
- norm_gain: float32 [128], replicated, may hold values from 0.1 to 1.9
- out_weight: bfloat16 [4096, 2048], P('tp'), may hold values from -0.09375 to 0.09375
Outputs:
- mixed: bfloat16 [8192, 2048], P(('ctx', 'tp'))
The draws below stay inside these ranges and needn't reach their ends.
Inputs may be any that keep to these rules, and one draw needn't show every extreme that they name: `log_decay`: strictly negative. `write_rate`: strictly between 0 and 1.
All inputs are finite; a program needn't handle non-finite values.
Results may differ from the reference program's by a relative error of at most 0.02.
Values may be sent and summed in bfloat16 or wider, within the bound.
No kernel may reach another device: no remote copies, remote signals or barrier semaphores. Data moves between devices by JAX's collectives and lax.ppermute only.
A program may use at most 128 MiB of HBM per device.

```python
import math
import jax
import jax.numpy as jnp
from jax import lax

D = 2048
VALUE_HEADS = 32
DK = 128
DV = 128
TOK_DEV = 256
SEQUENCE_TOKENS = 8192
N_TP = 8


def shared_directions(key):
    return jnp.clip(jax.random.normal(jax.random.fold_in(key, 5), (VALUE_HEADS, DK), jnp.float32), -4.0, 4.0)


def head_classes(key, slow_count):
    ranking = jax.random.permutation(jax.random.fold_in(key, 7), VALUE_HEADS)
    medium_count = (VALUE_HEADS - slow_count) // 2
    slow_mask = ranking < slow_count
    medium_mask = (ranking >= slow_count) & (ranking < slow_count + medium_count)
    return (slow_mask, medium_mask)


def coherent_rows(common, weight, jitter):
    mixed_rows = weight * common[None, :, :] + jitter
    return jnp.clip(mixed_rows, -8.0, 8.0).reshape(SEQUENCE_TOKENS, VALUE_HEADS * DK).astype(jnp.bfloat16)


def draw_queries(key, part):
    common = shared_directions(key)
    key = jax.random.fold_in(key, 37)
    key_list = jax.random.split(key, 2)
    weight = jax.random.uniform(key_list[0], (SEQUENCE_TOKENS, VALUE_HEADS, 1), jnp.float32, 0.4, 0.8)
    jitter = jnp.clip(jax.random.normal(key_list[1], (SEQUENCE_TOKENS, VALUE_HEADS, DK), jnp.float32), -6.0, 6.0)
    return coherent_rows(common, weight, jitter)


def draw_key_rows(key, part):
    common = shared_directions(key)
    key = jax.random.fold_in(key, 31)
    key_list = jax.random.split(key, 2)
    weight = jax.random.uniform(key_list[0], (SEQUENCE_TOKENS, VALUE_HEADS, 1), jnp.float32, 0.7, 1.3)
    jitter = jnp.clip(jax.random.normal(key_list[1], (SEQUENCE_TOKENS, VALUE_HEADS, DK), jnp.float32), -6.0, 6.0)
    return coherent_rows(common, weight, jitter)


def draw_log_decay(key, part):
    slow_count = VALUE_HEADS // 2
    slow_mask, medium_mask = head_classes(key, slow_count)
    key = jax.random.fold_in(key, 11)
    key_list = jax.random.split(key, 8)
    half_log = math.log(2.0)
    shard_count = SEQUENCE_TOKENS // TOK_DEV
    fast_rate = jnp.exp(jax.random.uniform(key_list[0], (VALUE_HEADS, 1), jnp.float32, math.log(1.0 / 50.0), math.log(1.0 / 30.0)))
    slow_rate = 0.2 / SEQUENCE_TOKENS * jnp.exp(jax.random.uniform(key_list[1], (VALUE_HEADS, 1), jnp.float32, -half_log, half_log))
    medium_rate = jax.random.uniform(key_list[2], (VALUE_HEADS, 1), jnp.float32, 2.3, 2.6) * (half_log / (0.75 * TOK_DEV))
    head_rate = jnp.where(slow_mask[:, None], slow_rate, jnp.where(medium_mask[:, None], medium_rate, fast_rate))
    token_multiplier = jnp.exp(jax.random.uniform(key_list[3], (VALUE_HEADS, SEQUENCE_TOKENS), jnp.float32, -half_log, half_log))
    wide_shard = jnp.exp(jax.random.uniform(key_list[4], (VALUE_HEADS, shard_count), jnp.float32, -half_log, half_log))
    narrow_shard = jnp.exp(jax.random.uniform(key_list[5], (VALUE_HEADS, shard_count), jnp.float32, -0.05, 0.05))
    shard_multiplier = jnp.repeat(jnp.where(medium_mask[:, None], narrow_shard, wide_shard), TOK_DEV, axis=1)
    spike_position = jax.random.randint(key_list[6], (3,), 0, SEQUENCE_TOKENS)
    spike_mask = jnp.any(jnp.arange(SEQUENCE_TOKENS)[None, :] == spike_position[:, None], axis=0)
    spike_penalty = jnp.log(jax.random.uniform(key_list[7], (VALUE_HEADS, SEQUENCE_TOKENS), jnp.float32, 0.55, 0.8))
    return -head_rate * token_multiplier * shard_multiplier + jnp.where(spike_mask[None, :], spike_penalty, 0.0)


def draw_write_rate(key, part):
    slow_count = VALUE_HEADS // 2
    slow_mask, medium_mask = head_classes(key, slow_count)
    key = jax.random.fold_in(key, 23)
    key_list = jax.random.split(key, 3)
    fast_write = jax.random.uniform(key_list[0], (VALUE_HEADS, SEQUENCE_TOKENS), jnp.float32, 0.2, 0.9)
    medium_write = jax.random.uniform(key_list[1], (VALUE_HEADS, SEQUENCE_TOKENS), jnp.float32, 0.1, 0.4)
    slow_write = 1.2 * DK / SEQUENCE_TOKENS * jnp.exp(jax.random.uniform(key_list[2], (VALUE_HEADS, SEQUENCE_TOKENS), jnp.float32, -0.15, 0.15))
    return jnp.where(slow_mask[:, None], slow_write, jnp.where(medium_mask[:, None], medium_write, fast_write))


def shard_levels(stream_key, shape, cuts, smallest, top_value):
    gain = 1.0
    for position, shards_of in cuts:
        draws = jax.random.uniform(jax.random.fold_in(jax.random.fold_in(stream_key, 6), position), (shards_of,), jnp.float32, smallest / len(cuts), top_value / len(cuts))
        gain = gain * jnp.repeat(jnp.exp(draws), shape[position] // shards_of).reshape((-1,) + (1,) * (len(shape) - 1 - position))
    return gain


def scatter_about(stream_key, dims, scale, limit, cuts=(), kind=jnp.bfloat16):
    level = shard_levels(stream_key, dims, cuts, -0.22, 0.18) if cuts else 1.0
    result = jax.random.normal(stream_key, dims, jnp.float32) * scale * level
    return jnp.minimum(jnp.maximum(result, -limit), limit).astype(kind)


def setup_inputs(seed: int = 0) -> dict:
    arg_keys = jax.random.split(jax.random.key(seed), 9)
    queries = draw_queries(jax.random.fold_in(arg_keys[8], 71), 0)
    key_rows = draw_key_rows(jax.random.fold_in(arg_keys[8], 71), 0)
    value_rows = scatter_about(arg_keys[2], (SEQUENCE_TOKENS, VALUE_HEADS * DV), 1.0, 6.0, ((0, 32), (1, 8)))
    log_decay = draw_log_decay(jax.random.fold_in(arg_keys[8], 71), 0)
    write_rate = draw_write_rate(jax.random.fold_in(arg_keys[8], 71), 0)
    gate_input = scatter_about(arg_keys[5], (SEQUENCE_TOKENS, VALUE_HEADS * DV), 1.0, 6.0, ((0, 32), (1, 8)))
    norm_gain = jnp.clip(1.0 + 0.18 * jax.random.normal(arg_keys[6], (DV,), jnp.float32), 0.1, 1.9)
    out_weight = scatter_about(arg_keys[7], (VALUE_HEADS * DV, D), (VALUE_HEADS * DV) ** -0.5, 0.09375, ((0, 8),))
    return dict(queries=queries, key_rows=key_rows, value_rows=value_rows, log_decay=log_decay, write_rate=write_rate, gate_input=gate_input, norm_gain=norm_gain, out_weight=out_weight)


highest = lax.Precision.HIGHEST
block_rows = 64
epsilon = 1e-06

def unit_rows(values):
    return values / jnp.sqrt(lax.optimization_barrier(jnp.sum(values * values, axis=-1, keepdims=True)) + epsilon)

def block_terms(query_raw, key_raw, value_raw, log_steps, write_steps):
    key_width = key_raw.shape[-1]
    query_rows = unit_rows(query_raw.astype(jnp.float32)) * key_width ** (-0.5)
    key_rows = unit_rows(key_raw.astype(jnp.float32))
    value_rows = value_raw.astype(jnp.float32)
    length = query_rows.shape[-2]
    log_gamma = jnp.cumsum(log_steps, axis=-1)
    decays = jnp.exp(log_gamma)
    later_pos = jnp.arange(length)[:, None]
    earlier_pos = jnp.arange(length)[None, :]
    inclusive = later_pos >= earlier_pos
    strictly = later_pos > earlier_pos
    spread = log_gamma[..., :, None] - log_gamma[..., None, :]
    weights = jnp.where(inclusive, jnp.exp(jnp.where(inclusive, spread, 0.0)), 0.0)
    key_intersection = jnp.einsum('...cd,...sd->...cs', key_rows, key_rows, precision=highest)
    system = jnp.eye(length, dtype=jnp.float32) + write_steps[..., :, None] * jnp.where(strictly, weights * key_intersection, 0.0)
    right_side = jnp.concatenate([write_steps[..., None] * value_rows, (write_steps * decays)[..., None] * key_rows], axis=-1)
    solved = lax.linalg.triangular_solve(system, right_side, left_side=True, lower=True, unit_diagonal=True)
    value_width = value_rows.shape[-1]
    new_values = solved[..., :value_width]
    erasers = solved[..., value_width:]
    scores = weights * jnp.einsum('...cd,...sd->...cs', query_rows, key_rows, precision=highest)
    local_out = jnp.einsum('...cs,...se->...ce', scores, new_values, precision=highest)
    query_map = decays[..., None] * query_rows - jnp.einsum('...cs,...sd->...cd', scores, erasers, precision=highest)
    weighted = jnp.exp(log_gamma[..., -1:] - log_gamma)[..., None] * key_rows
    transit = decays[..., -1][..., None, None] * jnp.eye(key_width, dtype=jnp.float32) - jnp.einsum('...cd,...ce->...de', weighted, erasers, precision=highest)
    state_add = jnp.einsum('...cd,...ce->...de', weighted, new_values, precision=highest)
    return (local_out, query_map, transit, state_add)

def to_blocks(values, heads):
    total = values.shape[0]
    return values.reshape(total // block_rows, block_rows, heads, values.shape[1] // heads).transpose(0, 2, 1, 3)

def rates_to_blocks(values):
    heads, total = values.shape
    return values.reshape(heads, total // block_rows, block_rows).transpose(1, 0, 2)

def gated_rows(core, gate_input, norm_gain):
    total, heads, width = core.shape
    normed = core / jnp.sqrt(lax.optimization_barrier(jnp.mean(core * core, axis=-1, keepdims=True)) + epsilon)
    gate_values = gate_input.astype(jnp.float32).reshape(total, heads, width)
    return (normed * norm_gain * jax.nn.silu(gate_values)).astype(jnp.bfloat16).reshape(total, heads * width)

def reference(queries, key_rows, value_rows, log_decay, write_rate, gate_input, norm_gain, out_weight):
    heads = log_decay.shape[0]
    total = queries.shape[0]
    blocks = (to_blocks(queries, heads), to_blocks(key_rows, heads), to_blocks(value_rows, heads), rates_to_blocks(log_decay), rates_to_blocks(write_rate))

    def advance(state_in, block):
        local_out, query_map, transit, state_add = block_terms(*block)
        out_rows = local_out + jnp.einsum('hcd,hde->hce', query_map, state_in, precision=highest)
        state_next = jnp.einsum('hde,hef->hdf', transit, state_in, precision=highest) + state_add
        return (state_next, out_rows)
    start_state = jnp.zeros((heads, DK, DV), jnp.float32)
    _, core_blocks = lax.scan(advance, start_state, blocks)
    core = core_blocks.transpose(0, 2, 1, 3).reshape(total, heads, DV)
    gated = gated_rows(core, gate_input, norm_gain)
    group_width = VALUE_HEADS * DV // N_TP

    def add_group(group, running):
        first_col = (group * group_width).astype(jnp.int32)
        cols_part = lax.dynamic_slice_in_dim(gated, first_col, group_width, 1)
        rows_part = lax.dynamic_slice_in_dim(out_weight, first_col, group_width, 0)
        partial_value = jnp.dot(cols_part.astype(jnp.float32), rows_part.astype(jnp.float32), preferred_element_type=jnp.float32).astype(jnp.bfloat16)
        return running + lax.optimization_barrier(partial_value).astype(jnp.float32)
    summed = lax.fori_loop(jnp.int32(0), jnp.int32(N_TP), add_group, jnp.zeros((total, D), jnp.float32))
    return summed.astype(jnp.bfloat16)
```

```python
import jax
import jax.numpy as jnp
from jax import lax
from jax.experimental import pallas as pl
from jax.experimental.pallas import tpu as pltpu
from jax.sharding import PartitionSpec as P

F32 = jnp.float32
BF16 = jnp.bfloat16
EPS = 1e-6
HD = 128
C = 128
HPC = 2
NC = 4
NP = HPC * NC
SUB = 16


def dot(a, b):
    return lax.dot_general(a, b, (((1,), (0,)), ((), ())), preferred_element_type=F32)


def dot_nt(a, b):
    return lax.dot_general(a, b, (((1,), (1,)), ((), ())), preferred_element_type=F32)


def dot_tn(a, b):
    return lax.dot_general(a, b, (((0,), (0,)), ((), ())), preferred_element_type=F32)


def split(a):
    hi = a.astype(BF16)
    lo = (a - hi.astype(F32)).astype(BF16)
    return hi, lo


def lanes(*parts):
    return jnp.concatenate(parts, axis=1)


def rows(*parts):
    return jnp.concatenate(parts, axis=0)


def dot_sq(a, b):
    ah, al = split(a)
    bh, bl = split(b)
    out = dot(lanes(ah, al), rows(lanes(bh, bl), lanes(bh, jnp.zeros_like(bl))))
    return out[:, :C] + out[:, C:]


def dot_wide(a, b):
    ah, al = split(a)
    bh, bl = split(b)
    return dot(lanes(ah, al), rows(bh, bh)) + dot(ah, bl)


def dot_exact_left(a, b):
    bh, bl = split(b)
    out = dot(a, lanes(bh, bl))
    return out[:, :HD] + out[:, HD:]


def iota2(shape, dim):
    return lax.broadcasted_iota(jnp.int32, shape, dim)


def put_tokens(core, own, other, dst):
    half = own.shape[0]
    width = HPC * HD

    @pl.when(core == 0)
    def _():
        dst[:half, :] = own[:, :width]
        dst[half:, :] = other[:, :width]

    @pl.when(core != 0)
    def _():
        dst[:half, :] = other[:, width:]
        dst[half:, :] = own[:, width:]


def put_rates(core, own, other, dst):
    for h in range(HPC):
        for n in range(NC):
            p = h * NC + n
            s = slice((n % 2) * C, (n % 2) * C + C)

            @pl.when(core == 0)
            def _(h=h, n=n, p=p, s=s):
                src = own if n < 2 else other
                dst[p : p + 1, :] = src[h : h + 1, s]

            @pl.when(core != 0)
            def _(h=h, n=n, p=p, s=s):
                src = other if n < 2 else own
                dst[p : p + 1, :] = src[HPC + h : HPC + h + 1, s]


def maps_kernel(
    k_ref, ko_ref, v_ref, vo_ref, ld_ref, ldo_ref, wr_ref, wro_ref,
    ks_ref, wu_ref, vec_ref, vect_ref, map_ref, total_ref,
    vs, lds, wrs, xs, ts,
):
    core = lax.rem(lax.axis_index("ctx"), 2)
    put_tokens(core, k_ref, ko_ref, ks_ref)
    put_tokens(core, v_ref, vo_ref, vs)
    put_rates(core, ld_ref, ldo_ref, lds)
    put_rates(core, wr_ref, wro_ref, wrs)
    row = iota2((C, C), 0)
    col = iota2((C, C), 1)
    eye = row == col
    strict = row > col
    upper = (row <= col).astype(BF16)

    def keys(p):
        h, n = divmod(p, NC)
        return ks_ref[n * C : n * C + C, h * HD : h * HD + HD]

    def values(p):
        h, n = divmod(p, NC)
        return vs[n * C : n * C + C, h * HD : h * HD + HD]

    steps = lds[...]
    beta = wrs[...]
    s0 = steps.astype(BF16)
    r1 = steps - s0.astype(F32)
    s1 = r1.astype(BF16)
    s2 = (r1 - s1.astype(F32)).astype(BF16)
    g = dot(s0, upper) + (dot(s1, upper) + dot(s2, upper))
    gram = []
    norms = []
    for p in range(NP):
        kp = keys(p)
        kk = dot_nt(kp, kp)
        gram.append(kk)
        norms.append(jnp.sum(jnp.where(eye, kk, 0.0), axis=0, keepdims=True))
    rn = 1.0 / jnp.sqrt(rows(*norms) + EPS)
    eg = jnp.exp(g)
    gend = g[:, C - 1 : C]
    tail = jnp.exp(gend - g) * rn
    vec = rows(g, beta * rn, tail, rn, eg, beta * eg * rn, beta, beta)
    vec_ref[...] = vec
    vect = rows(vec, vec).T
    vect_ref[...] = vect[:, : NP * 8]

    def column(kind, p):
        i = kind * NP + p
        return vect[:, i : i + 1]

    lower = []
    for p in range(NP):
        spread = column(0, p) - g[p : p + 1, :]
        w = jnp.exp(jnp.where(strict, spread, 0.0))
        w = w * (column(1, p) * rn[p : p + 1, :]) * gram[p]
        lower.append(jnp.where(strict, w, 0.0))
    lane_block = lax.div(iota2((SUB, C), 1), SUB)
    for p in range(NP):
        acc = jnp.zeros((SUB, C), F32)
        for b in range(C // SUB):
            acc = acc + jnp.where(lane_block == b, lower[p][b * SUB : b * SUB + SUB, :], 0.0)
        xs[pl.ds(p, SUB, stride=NP), :] = acc
    base = row - SUB * lax.div(col, SUB)
    select = lanes(*[(base == j).astype(BF16) for j in range(SUB)])
    xh, xl = split(xs[...])
    spread_coef = dot(lanes(xh, xl), rows(select, select))
    lane_in = lax.rem(iota2((NP, C), 1), SUB)
    solved = []
    for i in range(SUB):
        acc = (lane_in == i).astype(F32)
        for j in range(i):
            acc = acc - spread_coef[i * NP : i * NP + NP, j * C : j * C + C] * solved[j]
        solved.append(acc)
        ts[i * NP : i * NP + NP, :] = acc
    inverse = []
    for p in range(NP):
        tp = ts[pl.ds(p, SUB, stride=NP), :]
        inverse.append(rows(*[jnp.where(lane_block == b, tp, 0.0) for b in range(C // SUB)]))
    size = SUB
    while size < C:
        rb = lax.div(row, size)
        cb = lax.div(col, size)
        mask = (rb == cb + 1) & (lax.rem(rb, 2) == 1)
        mids = [dot_sq(jnp.where(mask, lower[p], 0.0), inverse[p]) for p in range(NP)]
        inverse = [inverse[p] - dot_sq(inverse[p], mids[p]) for p in range(NP)]
        size *= 2
    maps = []
    for p in range(NP):
        h, n = divmod(p, NC)
        kp = keys(p)
        vp = values(p)
        eh, el = split(inverse[p] * vec[5 * NP + p : 5 * NP + p + 1, :])
        uh, ul = split(inverse[p] * beta[p : p + 1, :])
        erase = dot(lanes(eh, el), rows(kp, kp))
        write = dot(lanes(uh, ul), rows(vp, vp))
        both = lanes(erase, write)
        wu_ref[p] = both.astype(BF16)
        wh, wl = split(both * column(2, p))
        out = dot_tn(rows(kp, kp), rows(wh, wl))
        decay = jnp.where(eye, jnp.exp(gend[p : p + 1, :]), 0.0)
        m = lanes(decay - out[:, :HD], out[:, HD:])
        map_ref[p] = m
        maps.append(m)

    def follow(later, earlier):
        out = dot_wide(later[:, :HD], earlier)
        return lanes(out[:, :HD], out[:, HD:] + later[:, HD:])

    for h in range(HPC):
        m0, m1, m2, m3 = maps[h * NC : h * NC + NC]
        total_ref[h] = follow(follow(m3, m2), follow(m1, m0)).astype(BF16)


def reads_kernel(
    q_ref, qo_ref, ks_ref, wu_ref, vec_ref, vect_ref, map_ref, qeff_ref, local_ref, qs
):
    core = lax.rem(lax.axis_index("ctx"), 2)
    put_tokens(core, q_ref, qo_ref, qs)
    row = iota2((C, C), 0)
    col = iota2((C, C), 1)
    incl = row >= col
    scale = HD**-0.5
    vec = vec_ref[...]
    vect = vect_ref[...]

    def column(kind, p):
        i = kind * NP + p
        return vect[:, i : i + 1]

    def follow(later, earlier):
        out = dot_wide(later[:, :HD], earlier)
        return lanes(out[:, :HD], out[:, HD:] + later[:, HD:])

    for h in range(HPC):
        prefix = None
        for n in range(NC):
            p = h * NC + n
            qp = qs[n * C : n * C + C, h * HD : h * HD + HD]
            kp = ks_ref[n * C : n * C + C, h * HD : h * HD + HD]
            qf = qp.astype(F32)
            rq = scale / jnp.sqrt(jnp.sum(qf * qf, axis=1, keepdims=True) + EPS)
            w = jnp.exp(jnp.where(incl, column(0, p) - vec[p : p + 1, :], 0.0))
            scores = w * (rq * vec[3 * NP + p : 3 * NP + p + 1, :]) * dot_nt(qp, kp)
            sh, sl = split(jnp.where(incl, scores, 0.0))
            wu = wu_ref[p]
            out = dot(lanes(sh, sl), rows(wu, wu))
            qeff = (column(4, p) * rq) * qf - out[:, :HD]
            local = out[:, HD:]
            if n > 0:
                out = dot_wide(qeff, prefix)
                qeff = out[:, :HD]
                local = local + out[:, HD:]
            prefix = map_ref[p] if n == 0 else follow(map_ref[p], prefix)
            qeff_ref[h, n * C : n * C + C, :] = qeff.astype(BF16)
            local_ref[h, n * C : n * C + C, :] = local


def row_kernel(m_ref, r1_ref, r2_ref, r3_ref, total_ref, prefix_ref, slots):
    y = lax.rem(lax.div(lax.axis_index("ctx"), 2), 4)
    for d, ref in enumerate((m_ref, r1_ref, r2_ref, r3_ref)):
        slots[lax.rem(y + 4 - d, 4)] = ref[...]
    eye = (iota2((HD, 2 * HD), 0) == iota2((HD, 2 * HD), 1)).astype(F32)
    for h in range(HPC):
        m0, m1, m2, m3 = (slots[i, h] for i in range(4))
        b1, b2, b3 = (m[:, HD:].astype(F32) for m in (m1, m2, m3))
        t01 = dot(m1[:, :HD], m0)
        t01 = lanes(t01[:, :HD], t01[:, HD:] + b1)
        t23 = dot(m3[:, :HD], m2)
        t23 = lanes(t23[:, :HD], t23[:, HD:] + b3)
        th, tl = split(t01)
        t012 = dot(m2[:, :HD], th) + dot(m2[:, :HD], tl)
        t012 = lanes(t012[:, :HD], t012[:, HD:] + b2)
        total = dot_wide(t23[:, :HD], t01)
        total_ref[h] = lanes(total[:, :HD], total[:, HD:] + t23[:, HD:]).astype(BF16)
        prefix_ref[h] = jnp.where(
            y == 0, eye, jnp.where(y == 1, m0.astype(F32), jnp.where(y == 2, t01, t012))
        )


def gated_kernel(
    r1_ref, r2_ref, r3_ref, prefix_ref, qeff_ref, local_ref, gate_ref, gateo_ref, gain_ref,
    keep_ref, send_ref, gs,
):
    core = lax.rem(lax.axis_index("ctx"), 2)
    put_tokens(core, gate_ref, gateo_ref, gs)
    gain = gain_ref[...]
    half = gate_ref.shape[0]
    entering = []
    for h in range(HPC):
        state = r3_ref[h][:, HD:].astype(F32)
        for ref in (r2_ref, r1_ref):
            m = ref[h]
            state = dot_exact_left(m[:, :HD], state) + m[:, HD:].astype(F32)
        m = prefix_ref[h]
        state = dot_sq(m[:, :HD], state) + m[:, HD:]
        entering.append(split(state))
    for h in range(HPC):
        sh, sl = entering[h]
        out = dot(qeff_ref[h], lanes(sh, sl))
        core_rows = local_ref[h] + out[:, :HD] + out[:, HD:]
        mean = jnp.mean(core_rows * core_rows, axis=1, keepdims=True)
        gate = gs[:, h * HD : h * HD + HD].astype(F32)
        silu = gate / (1.0 + jnp.exp(-gate))
        out = (core_rows / jnp.sqrt(mean + EPS) * gain * silu).astype(BF16)
        s = slice(h * HD, h * HD + HD)

        @pl.when(core == 0)
        def _():
            keep_ref[:, s] = out[:half]
            send_ref[:, s] = out[half:]

        @pl.when(core != 0)
        def _():
            keep_ref[:, s] = out[half:]
            send_ref[:, s] = out[:half]


def project_kernel(keep_ref, recv_ref, w_ref, *refs):
    outs, lhs = refs[:-1], refs[-1]
    core = lax.rem(lax.axis_index("ctx"), 2)
    me = lax.axis_index("tp")
    width = HPC * HD
    chunk = 32
    for d in range(8):
        start = pl.multiple_of(lax.rem(me + d, 8) * chunk, chunk)
        here = slice(d * chunk, d * chunk + chunk)
        kept = keep_ref[pl.ds(start, chunk), :]
        got = recv_ref[pl.ds(start, chunk), :]

        @pl.when(core == 0)
        def _(here=here, kept=kept, got=got):
            lhs[here, :width] = kept
            lhs[here, width:] = got

        @pl.when(core != 0)
        def _(here=here, kept=kept, got=got):
            lhs[here, :width] = got
            lhs[here, width:] = kept

    step = 512
    for j in range(w_ref.shape[1] // step):
        s = slice(j * step, j * step + step)
        out = dot(lhs[...], w_ref[:, s]).astype(BF16)
        for d, ref in zip((0, 1, 2, 3, 5, 6, 7), (outs[0], outs[1], outs[2], outs[3], outs[6], outs[7], outs[8])):
            ref[:, s] = out[d * chunk : d * chunk + chunk]
        ref = outs[4] if j < 2 else outs[5]
        t = slice((j % 2) * step, (j % 2) * step + step)
        ref[:, t] = out[4 * chunk : 5 * chunk]


def partial_kernel(a_ref, a3_ref, a4_ref, b_ref, b3_ref, b4_ref, ao_ref, bo_ref):
    half = a4_ref.shape[1]
    a = a_ref[...].astype(F32) + a3_ref[...].astype(F32)
    b = b_ref[...].astype(F32) + b3_ref[...].astype(F32)
    ao_ref[:, :half] = (a[:, :half] + a4_ref[...].astype(F32)).astype(BF16)
    ao_ref[:, half:] = a[:, half:].astype(BF16)
    bo_ref[:, :half] = b[:, :half].astype(BF16)
    bo_ref[:, half:] = (b[:, half:] + b4_ref[...].astype(F32)).astype(BF16)


def sum_kernel(a_ref, b_ref, c_ref, d_ref, e_ref, out_ref):
    total = a_ref[...].astype(F32)
    for ref in (b_ref, c_ref, d_ref, e_ref):
        total = total + ref[...].astype(F32)
    out_ref[...] = total.astype(BF16)


def call(kernel, outs, args, scratch=(), flops=0, moved=0):
    vmem = pl.BlockSpec(memory_space=pltpu.VMEM)
    return pl.pallas_call(
        kernel,
        out_shape=[jax.ShapeDtypeStruct(s, t) for s, t in outs],
        in_specs=[vmem] * len(args),
        out_specs=[vmem] * len(outs),
        scratch_shapes=list(scratch),
        compiler_params=pltpu.CompilerParams(vmem_limit_bytes=32 * 1024 * 1024),
        cost_estimate=pl.CostEstimate(flops=flops, bytes_accessed=moved, transcendentals=0),
    )(*args)


def on_device(q, k, v, ld, wr, gate, gain, w):
    tokens = q.shape[0]
    chip = 2 * tokens
    ring = lax.axis_size("tp")
    n_ctx = lax.axis_size("ctx")
    cross = [(i, i ^ 1) for i in range(n_ctx)]

    def swap(a):
        return lax.ppermute(a, "ctx", cross)

    def along_y(a, d):
        pairs = []
        for i in range(n_ctx):
            x, y, c = i // 8, i // 2 % 4, i % 2
            pairs.append((i, (x * 4 + (y + d) % 4) * 2 + c))
        return lax.ppermute(a, "ctx", pairs)

    def along_x(a, d):
        return lax.ppermute(a, "ctx", [(i, i + 8 * d) for i in range(n_ctx - 8 * d)])

    def along_z(a, d):
        return lax.ppermute(a, "tp", [(i, (i + d) % ring) for i in range(ring)])

    ko, vo, ldo, wro = swap(k), swap(v), swap(ld), swap(wr)
    qo, gateo = swap(q), swap(gate)
    ks, wu, vec, vect, maps, total = call(
        maps_kernel,
        [
            ((chip, HPC * HD), BF16),
            ((NP, C, 2 * HD), BF16),
            ((8 * NP, C), F32),
            ((C, 8 * NP), F32),
            ((NP, HD, 2 * HD), F32),
            ((HPC, HD, 2 * HD), BF16),
        ],
        (k, ko, v, vo, ld, ldo, wr, wro),
        [
            pltpu.VMEM((chip, HPC * HD), BF16),
            pltpu.VMEM((NP, C), F32),
            pltpu.VMEM((NP, C), F32),
            pltpu.VMEM((SUB * NP, C), F32),
            pltpu.VMEM((SUB * NP, C), F32),
        ],
        flops=10**9,
        moved=2**20,
    )
    around = [along_y(total, d) for d in (1, 2, 3)]
    qeff, local = call(
        reads_kernel,
        [((HPC, chip, HD), BF16), ((HPC, chip, HD), F32)],
        (q, qo, ks, wu, vec, vect, maps),
        [pltpu.VMEM((chip, HPC * HD), BF16)],
        flops=10**9,
        moved=2**20,
    )
    row_total, prefix = call(
        row_kernel,
        [((HPC, HD, 2 * HD), BF16), ((HPC, HD, 2 * HD), F32)],
        (total, *around),
        [pltpu.VMEM((4, HPC, HD, 2 * HD), BF16)],
        flops=10**8,
        moved=2**19,
    )
    before = [along_x(row_total, d) for d in (1, 2, 3)]
    keep, send = call(
        gated_kernel,
        [((tokens, HPC * HD), BF16)] * 2,
        (*before, prefix, qeff, local, gate, gateo, gain.reshape(1, HD)),
        [pltpu.VMEM((chip, HPC * HD), BF16)],
        flops=10**8,
        moved=2**20,
    )
    recv = swap(send)
    width = w.shape[1]
    chunk = tokens // ring
    p0, p1, p2, p3, p4a, p4b, p5, p6, p7 = call(
        project_kernel,
        [((chunk, width), BF16)] * 4 + [((chunk, width // 2), BF16)] * 2 + [((chunk, width), BF16)] * 3,
        (keep, recv, w),
        [pltpu.VMEM((tokens, w.shape[0]), BF16)],
        flops=10**9,
        moved=2**22,
    )
    a3, b3 = along_z(p3, 1), along_z(p5, -1)
    a4, b4 = along_z(p4a, 2), along_z(p4b, -2)
    a1, b1 = along_z(p1, 1), along_z(p7, -1)
    pa, pb = call(partial_kernel, [((chunk, width), BF16)] * 2, (p2, a3, a4, p6, b3, b4))
    a2, b2 = along_z(pa, 2), along_z(pb, -2)
    return call(sum_kernel, [((chunk, width), BF16)], (p0, a1, b1, a2, b2))[0]


def solution(mesh):
    in_specs = (
        P("ctx", "tp"),
        P("ctx", "tp"),
        P("ctx", "tp"),
        P("tp", "ctx"),
        P("tp", "ctx"),
        P("ctx", "tp"),
        P(),
        P("tp", None),
    )
    return jax.shard_map(
        on_device, mesh=mesh, in_specs=in_specs, out_specs=P(("ctx", "tp"), None), check_vma=False
    )
```

```python
import jax
import jax.numpy as jnp
from jax import lax
from jax.experimental import pallas as pl
from jax.experimental.pallas import tpu as pltpu
from jax.sharding import PartitionSpec as P

F32 = jnp.float32
BF16 = jnp.bfloat16
EPS = 1e-6
HD = 128
C = 128
HEADS = 4
OWN = 2
NC = 2
NP = HEADS * NC
SUB = 16
TP = 8


def dot(a, b):
    return lax.dot_general(a, b, (((1,), (0,)), ((), ())), preferred_element_type=F32)


def dot_nt(a, b):
    return lax.dot_general(a, b, (((1,), (1,)), ((), ())), preferred_element_type=F32)


def dot_tn(a, b):
    return lax.dot_general(a, b, (((0,), (0,)), ((), ())), preferred_element_type=F32)


def split(a):
    hi = a.astype(BF16)
    lo = (a - hi.astype(F32)).astype(BF16)
    return hi, lo


def lanes(*parts):
    return jnp.concatenate(parts, axis=1)


def rows(*parts):
    return jnp.concatenate(parts, axis=0)


def dot_sq(a, b):
    ah, al = split(a)
    bh, bl = split(b)
    out = dot(lanes(ah, al), rows(lanes(bh, bl), lanes(bh, jnp.zeros_like(bl))))
    return out[:, :C] + out[:, C:]


def dot_wide(a, b):
    ah, al = split(a)
    bh, bl = split(b)
    return dot(lanes(ah, al), rows(bh, bh)) + dot(ah, bl)


def dot_exact_left(a, b):
    bh, bl = split(b)
    out = dot(a, lanes(bh, bl))
    return out[:, :HD] + out[:, HD:]


def follow(later, earlier):
    out = dot_wide(later[:, :HD], earlier)
    return lanes(out[:, :HD], out[:, HD:] + later[:, HD:])


def iota2(shape, dim):
    return lax.broadcasted_iota(jnp.int32, shape, dim)


def core_index():
    return lax.rem(lax.axis_index("ctx"), 2)


def part(ref, p):
    n, h = divmod(p, HEADS)
    return ref[n * C : n * C + C, h * HD : h * HD + HD]


def maps_kernel(
    k_hbm, v_hbm, ld_hbm, wr_hbm,
    wu_ref, vec_ref, vect_ref, first_ref, keep_ref, send_ref,
    k_ref, v_ref, ld_ref, wr_ref, xs, ts, sems,
):
    copies = [
        pltpu.make_async_copy(src, dst, sems.at[i])
        for i, (src, dst) in enumerate(
            ((ld_hbm, ld_ref), (wr_hbm, wr_ref), (k_hbm, k_ref), (v_hbm, v_ref))
        )
    ]
    for copy in copies:
        copy.start()
    core = core_index()
    row = iota2((C, C), 0)
    col = iota2((C, C), 1)
    eye = row == col
    strict = row > col
    upper = (row <= col).astype(BF16)
    base = row - SUB * lax.div(col, SUB)
    select = lanes(*[(base == j).astype(BF16) for j in range(SUB)])
    for copy in copies[:3]:
        copy.wait()
    steps = rows(ld_ref[:, :C], ld_ref[:, C:])
    beta = rows(wr_ref[:, :C], wr_ref[:, C:])
    s0 = steps.astype(BF16)
    r1 = steps - s0.astype(F32)
    s1 = r1.astype(BF16)
    s2 = (r1 - s1.astype(F32)).astype(BF16)
    g = dot(s0, upper) + (dot(s1, upper) + dot(s2, upper))
    gram = []
    norms = []
    for p in range(NP):
        kp = part(k_ref, p)
        kk = dot_nt(kp, kp)
        gram.append(kk)
        norms.append(jnp.sum(jnp.where(eye, kk, 0.0), axis=0, keepdims=True))
    rn = 1.0 / jnp.sqrt(rows(*norms) + EPS)
    eg = jnp.exp(g)
    gend = g[:, C - 1 : C]
    tail = jnp.exp(gend - g) * rn
    vec = rows(g, beta * rn, tail, rn, eg, beta * eg * rn, beta, beta)
    vec_ref[...] = vec
    vect = rows(vec, vec).T
    vect_ref[...] = vect[:, : NP * 8]

    def column(kind, p):
        i = kind * NP + p
        return vect[:, i : i + 1]

    lower = []
    for p in range(NP):
        spread = column(0, p) - g[p : p + 1, :]
        w = jnp.exp(jnp.where(strict, spread, 0.0))
        w = w * (column(1, p) * rn[p : p + 1, :]) * gram[p]
        lower.append(jnp.where(strict, w, 0.0))
    lane_block = lax.div(iota2((SUB, C), 1), SUB)
    for p in range(NP):
        acc = jnp.zeros((SUB, C), F32)
        for b in range(C // SUB):
            acc = acc + jnp.where(lane_block == b, lower[p][b * SUB : b * SUB + SUB, :], 0.0)
        xs[pl.ds(p, SUB, stride=NP), :] = acc
    xh, xl = split(xs[...])
    coef = dot(lanes(xh, xl), rows(select, select))
    lane_in = lax.rem(iota2((NP, C), 1), SUB)
    solved = []
    for i in range(SUB):
        acc = (lane_in == i).astype(F32)
        for j in range(i):
            acc = acc - coef[i * NP : i * NP + NP, j * C : j * C + C] * solved[j]
        solved.append(acc)
        ts[i * NP : i * NP + NP, :] = acc
    inverse = []
    for p in range(NP):
        tp = ts[pl.ds(p, SUB, stride=NP), :]
        inverse.append(rows(*[jnp.where(lane_block == b, tp, 0.0) for b in range(C // SUB)]))
    size = SUB
    while size < C:
        rb = lax.div(row, size)
        cb = lax.div(col, size)
        mask = (rb == cb + 1) & (lax.rem(rb, 2) == 1)
        mids = [dot_sq(jnp.where(mask, lower[p], 0.0), inverse[p]) for p in range(NP)]
        inverse = [inverse[p] - dot_sq(inverse[p], mids[p]) for p in range(NP)]
        size *= 2
    copies[3].wait()
    maps = []
    for p in range(NP):
        kp = part(k_ref, p)
        vp = part(v_ref, p)
        eh, el = split(inverse[p] * vec[5 * NP + p : 5 * NP + p + 1, :])
        uh, ul = split(inverse[p] * beta[p : p + 1, :])
        erase = dot(lanes(eh, el), rows(kp, kp))
        write = dot(lanes(uh, ul), rows(vp, vp))
        both = lanes(erase, write)
        wu_ref[p] = both.astype(BF16)
        wh, wl = split(both * column(2, p))
        out = dot_tn(rows(kp, kp), rows(wh, wl))
        decay = jnp.where(eye, jnp.exp(gend[p : p + 1, :]), 0.0)
        maps.append(lanes(decay - out[:, :HD], out[:, HD:]))
    whole = []
    for h in range(HEADS):
        first_ref[h] = maps[h]
        whole.append(follow(maps[HEADS + h], maps[h]))
    for h in range(OWN):
        keep_ref[h] = jnp.where(core == 0, whole[h], whole[OWN + h])
        send_ref[h] = jnp.where(core == 0, whole[OWN + h], whole[h]).astype(BF16)


def pair_kernel(keep_ref, recv_ref, total_ref, early_ref):
    core = core_index()
    for h in range(OWN):
        mine = keep_ref[h]
        other = recv_ref[h].astype(F32)
        early = jnp.where(core == 0, mine, other)
        late = jnp.where(core == 0, other, mine)
        early_ref[h] = early
        total_ref[h] = follow(late, early).astype(BF16)


def reads_kernel(q_ref, k_ref, wu_ref, vec_ref, vect_ref, first_ref, qeff_ref, local_ref):
    row = iota2((C, C), 0)
    col = iota2((C, C), 1)
    incl = row >= col
    scale = HD**-0.5
    vec = vec_ref[...]
    vect = vect_ref[...]

    def column(kind, p):
        i = kind * NP + p
        return vect[:, i : i + 1]

    for p in range(NP):
        n, h = divmod(p, HEADS)
        qp = part(q_ref, p)
        qf = qp.astype(F32)
        rq = scale / jnp.sqrt(jnp.sum(qf * qf, axis=1, keepdims=True) + EPS)
        w = jnp.exp(jnp.where(incl, column(0, p) - vec[p : p + 1, :], 0.0))
        scores = w * (rq * vec[3 * NP + p : 3 * NP + p + 1, :]) * dot_nt(qp, part(k_ref, p))
        sh, sl = split(jnp.where(incl, scores, 0.0))
        wu = wu_ref[p]
        out = dot(lanes(sh, sl), rows(wu, wu))
        qeff = (column(4, p) * rq) * qf - out[:, :HD]
        local = out[:, HD:]
        if n > 0:
            out = dot_wide(qeff, first_ref[h])
            qeff = out[:, :HD]
            local = local + out[:, HD:]
        qeff_ref[h, n * C : n * C + C, :] = qeff.astype(BF16)
        local_ref[h, n * C : n * C + C, :] = local


def y_index():
    return lax.rem(lax.div(lax.axis_index("ctx"), 2), 4)


def x_index():
    return lax.div(lax.axis_index("ctx"), 8)


def follow_sent(later, earlier):
    out = dot(later[:, :HD], earlier)
    return lanes(out[:, :HD], out[:, HD:] + later[:, HD:].astype(F32))


def two_kernel(m_ref, recv_ref, after, two_ref):
    del after
    odd = lax.rem(y_index(), 2) == 1
    for h in range(OWN):
        mine, other = m_ref[h], recv_ref[h]
        early = jnp.where(odd, other, mine)
        late = jnp.where(odd, mine, other)
        two_ref[h] = follow_sent(late, early).astype(BF16)


def row_kernel(recv_ref, two_ref, recv_two_ref, total_ref, prefix_ref):
    y = y_index()
    eye = (iota2((HD, 2 * HD), 0) == iota2((HD, 2 * HD), 1)).astype(F32)
    for h in range(OWN):
        mine, other = two_ref[h], recv_two_ref[h]
        early = jnp.where(y >= 2, other, mine)
        late = jnp.where(y >= 2, mine, other)
        total_ref[h] = follow_sent(late, early).astype(BF16)
        before = recv_ref[h]
        prefix_ref[h] = jnp.where(
            y == 0,
            eye,
            jnp.where(
                y == 1,
                before.astype(F32),
                jnp.where(y == 2, early.astype(F32), follow_sent(before, early)),
            ),
        )


def half_kernel(m_ref, recv_ref, add_ref):
    odd = lax.rem(x_index(), 2) == 1
    for h in range(OWN):
        mine, other = m_ref[h], recv_ref[h]
        early = jnp.where(odd, other, mine)
        late = jnp.where(odd, mine, other)
        out = dot(late[:, :HD], early[:, HD:]) + late[:, HD:].astype(F32)
        add_ref[h] = out.astype(BF16)


def state_kernel(recv_ref, half_ref, prefix_ref, early_ref, keep_ref, send_ref):
    core = core_index()
    x = x_index()
    for h in range(OWN):
        m = recv_ref[h]
        half = half_ref[h]
        through = dot(m[:, :HD], half)
        state = jnp.where(x >= 2, half.astype(F32), 0.0)
        state = jnp.where(x == 3, through, state)
        state = state + jnp.where(lax.rem(x, 2) == 1, m[:, HD:].astype(F32), 0.0)
        for_cores = []
        for ref in (prefix_ref, early_ref):
            m = ref[h]
            state = dot_sq(m[:, :HD], state) + m[:, HD:]
            for_cores.append(state)
        hi, lo = split(jnp.where(core == 0, for_cores[0], for_cores[1]))
        keep_ref[h] = lanes(hi, lo)
        send_ref[h] = jnp.where(core == 0, for_cores[1], for_cores[0]).astype(BF16)


def gated_rows(state, head, qeff_ref, local_ref, gate_ref, gain):
    out = dot(qeff_ref[head], state)
    core_rows = local_ref[head] + out[:, :HD]
    if state.shape[1] > HD:
        core_rows = core_rows + out[:, HD:]
    mean = jnp.mean(core_rows * core_rows, axis=1, keepdims=True)
    gate = gate_ref[:, pl.ds(pl.multiple_of(head * HD, HD), HD)].astype(F32)
    silu = gate / (1.0 + jnp.exp(-gate))
    return (core_rows / jnp.sqrt(mean + EPS) * gain * silu).astype(BF16)


def gather_rows(state_ref, first, qeff_ref, local_ref, gate_ref, gain_ref, gs, lhs):
    for h in range(OWN):
        gs[:, h * HD : h * HD + HD] = gated_rows(
            state_ref[h], first + h, qeff_ref, local_ref, gate_ref, gain_ref[...]
        )
    me = lax.axis_index("tp")
    chunk = gs.shape[0] // TP
    for d in range(TP):
        start = pl.multiple_of(lax.rem(me + d, TP) * chunk, chunk)
        lhs[d * chunk : d * chunk + chunk, :] = gs[pl.ds(start, chunk), :]


def weight_rows(w_ref, first, s):
    return w_ref[pl.ds(pl.multiple_of(first * HD, OWN * HD), OWN * HD), s]


STEP = 512


def own_kernel(state_ref, qeff_ref, local_ref, gate_ref, gain_ref, w_ref, acc_ref, gs, lhs):
    first = OWN * core_index()
    gather_rows(state_ref, first, qeff_ref, local_ref, gate_ref, gain_ref, gs, lhs)
    for j in range(w_ref.shape[1] // STEP):
        s = slice(j * STEP, j * STEP + STEP)
        acc_ref[:, s] = dot(lhs[...], weight_rows(w_ref, first, s))


def other_kernel(
    state_ref, acc_ref, qeff_ref, local_ref, gate_ref, gain_ref, w_ref, *refs
):
    outs, (gs, lhs) = refs[:-2], refs[-2:]
    first = OWN * (1 - core_index())
    gather_rows(state_ref, first, qeff_ref, local_ref, gate_ref, gain_ref, gs, lhs)
    chunk = gs.shape[0] // TP
    for j in range(w_ref.shape[1] // STEP):
        s = slice(j * STEP, j * STEP + STEP)
        out = (acc_ref[:, s] + dot(lhs[...], weight_rows(w_ref, first, s))).astype(BF16)
        for d, ref in zip((0, 1, 2, 3, 5, 6, 7), outs):
            ref[:, s] = out[d * chunk : d * chunk + chunk]
        ref = outs[7 + j // 2]
        t = slice(j % 2 * STEP, j % 2 * STEP + STEP)
        ref[:, t] = out[4 * chunk : 5 * chunk]


def partial_kernel(a_ref, a3_ref, a4_ref, b_ref, b3_ref, b4_ref, ao_ref, bo_ref):
    half = a4_ref.shape[1]
    a = a_ref[...].astype(F32) + a3_ref[...].astype(F32)
    b = b_ref[...].astype(F32) + b3_ref[...].astype(F32)
    ao_ref[:, :half] = (a[:, :half] + a4_ref[...].astype(F32)).astype(BF16)
    ao_ref[:, half:] = a[:, half:].astype(BF16)
    bo_ref[:, :half] = b[:, :half].astype(BF16)
    bo_ref[:, half:] = (b[:, half:] + b4_ref[...].astype(F32)).astype(BF16)


def sum_kernel(*refs):
    total = refs[0][...].astype(F32)
    for ref in refs[1:-1]:
        total = total + ref[...].astype(F32)
    refs[-1][...] = total.astype(BF16)


def call(kernel, outs, args, scratch=(), hbm=(), flops=10**8, moved=2**20, vmem_mib=32):
    vmem = pl.BlockSpec(memory_space=pltpu.VMEM)
    stay = pl.BlockSpec(memory_space=pltpu.HBM)
    loose = pl.BlockSpec(memory_space=pl.ANY)
    specs = [{"hbm": stay, "any": loose}.get(dict(hbm).get(i), vmem) for i in range(len(args))]
    return pl.pallas_call(
        kernel,
        out_shape=[jax.ShapeDtypeStruct(s, t) for s, t in outs],
        in_specs=specs,
        out_specs=[vmem] * len(outs),
        scratch_shapes=list(scratch),
        compiler_params=pltpu.CompilerParams(vmem_limit_bytes=vmem_mib * 2**20),
        cost_estimate=pl.CostEstimate(flops=flops, bytes_accessed=moved, transcendentals=0),
    )(*args)


def on_device(q, k, v, ld, wr, gate, gain, w):
    tokens = q.shape[0]
    n_ctx = lax.axis_size("ctx")

    def swap(a):
        return lax.ppermute(a, "ctx", [(i, i ^ 1) for i in range(n_ctx)])

    def across_y(a, m):
        pairs = [(i, (i // 8 * 4 + (i // 2 % 4 ^ m)) * 2 + i % 2) for i in range(n_ctx)]
        return lax.ppermute(a, "ctx", pairs)

    def across_x(a, m):
        return lax.ppermute(a, "ctx", [(i, (i // 8 ^ m) * 8 + i % 8) for i in range(n_ctx)])

    def along_z(a, d):
        return lax.ppermute(a, "tp", [(i, (i + d) % TP) for i in range(TP)])

    pair = (OWN, HD, 2 * HD)
    wu, vec, vect, first, keep, send = call(
        maps_kernel,
        [
            ((NP, C, 2 * HD), BF16),
            ((8 * NP, C), F32),
            ((C, 8 * NP), F32),
            ((HEADS, HD, 2 * HD), F32),
            (pair, F32),
            (pair, BF16),
        ],
        tuple(pltpu.with_memory_space_constraint(a, pltpu.HBM) for a in (k, v, ld, wr)),
        [
            pltpu.VMEM(k.shape, BF16),
            pltpu.VMEM(v.shape, BF16),
            pltpu.VMEM(ld.shape, F32),
            pltpu.VMEM(wr.shape, F32),
            pltpu.VMEM((SUB * NP, C), F32),
            pltpu.VMEM((SUB * NP, C), F32),
            pltpu.SemaphoreType.DMA((4,)),
        ],
        hbm={0: "hbm", 1: "hbm", 2: "hbm", 3: "hbm"},
        flops=10**9,
        vmem_mib=32,
    )
    total, early = call(pair_kernel, [(pair, BF16), (pair, F32)], (keep, swap(send)))
    beside = across_y(total, 1)
    qeff, local = call(
        reads_kernel,
        [((HEADS, tokens, HD), BF16), ((HEADS, tokens, HD), F32)],
        (q, k, wu, vec, vect, first),
        flops=10**9,
    )
    (two,) = call(two_kernel, [(pair, BF16)], (total, beside, local), hbm={2: "any"})
    row_total, prefix = call(
        row_kernel, [(pair, BF16), (pair, F32)], (beside, two, across_y(two, 3))
    )
    beside_row = across_x(row_total, 1)
    (half,) = call(half_kernel, [((OWN, HD, HD), BF16)], (row_total, beside_row))
    own_state, send_state = call(
        state_kernel,
        [(pair, BF16), ((OWN, HD, HD), BF16)],
        (beside_row, across_x(half, 3), prefix, early),
    )
    other_state = swap(send_state)
    gain = gain.reshape(1, HD)
    rows_scratch = [pltpu.VMEM((tokens, OWN * HD), BF16)] * 2
    width = w.shape[1]
    (acc,) = call(
        own_kernel,
        [((tokens, width), F32)],
        (own_state, qeff, local, gate, gain, w),
        rows_scratch,
        flops=10**9,
    )
    rows_here = tokens // TP
    block = ((rows_here, width), BF16)
    p0, p1, p2, p3, p5, p6, p7, p4a, p4b = call(
        other_kernel,
        [block] * 7 + [((rows_here, width // 2), BF16)] * 2,
        (other_state, acc, qeff, local, gate, gain, w),
        rows_scratch,
        flops=10**9,
    )
    a3, b3 = along_z(p3, 1), along_z(p5, -1)
    a4, b4 = along_z(p4a, 2), along_z(p4b, -2)
    a1, b1 = along_z(p1, 1), along_z(p7, -1)
    pa, pb = call(partial_kernel, [block] * 2, (p2, a3, a4, p6, b3, b4))
    a2, b2 = along_z(pa, 2), along_z(pb, -2)
    return call(sum_kernel, [block], (p0, a1, b1, a2, b2))[0]


def solution(mesh):
    in_specs = (
        P("ctx", "tp"),
        P("ctx", "tp"),
        P("ctx", "tp"),
        P("tp", "ctx"),
        P("tp", "ctx"),
        P("ctx", "tp"),
        P(),
        P("tp", None),
    )
    return jax.shard_map(
        on_device, mesh=mesh, in_specs=in_specs, out_specs=P(("ctx", "tp"), None), check_vma=False
    )
```

```python
import jax
import jax.numpy as jnp
from jax import lax
from jax.experimental import pallas as pl
from jax.experimental.pallas import tpu as pltpu
from jax.sharding import PartitionSpec as P

F32 = jnp.float32
BF16 = jnp.bfloat16
EPS = 1e-6
HD = 128
C = 128
HEADS = 4
OWN = 2
NC = 2
NP = HEADS * NC
SUB = 16
TP = 8


def dot(a, b):
    return lax.dot_general(a, b, (((1,), (0,)), ((), ())), preferred_element_type=F32)


def dot_nt(a, b):
    return lax.dot_general(a, b, (((1,), (1,)), ((), ())), preferred_element_type=F32)


def dot_tn(a, b):
    return lax.dot_general(a, b, (((0,), (0,)), ((), ())), preferred_element_type=F32)


def split(a):
    hi = a.astype(BF16)
    lo = (a - hi.astype(F32)).astype(BF16)
    return hi, lo


def lanes(*parts):
    return jnp.concatenate(parts, axis=1)


def rows(*parts):
    return jnp.concatenate(parts, axis=0)


def dot_sq(a, b):
    ah, al = split(a)
    bh, bl = split(b)
    out = dot(lanes(ah, al), rows(lanes(bh, bl), lanes(bh, jnp.zeros_like(bl))))
    return out[:, :C] + out[:, C:]


def dot_wide(a, b):
    ah, al = split(a)
    bh, bl = split(b)
    return dot(lanes(ah, al), rows(bh, bh)) + dot(ah, bl)


def dot_exact_left(a, b):
    bh, bl = split(b)
    out = dot(a, lanes(bh, bl))
    return out[:, :HD] + out[:, HD:]


def follow(later, earlier):
    out = dot_wide(later[:, :HD], earlier)
    return lanes(out[:, :HD], out[:, HD:] + later[:, HD:])


def odd_rows(a, size):
    return rows(*[a[i : i + size] for i in range(size, C, 2 * size)])


def at_odd_rows(a, size):
    zero = jnp.zeros((size, a.shape[1]), a.dtype)
    out = []
    for i in range(0, C // 2, size):
        out += [zero, a[i : i + size]]
    return rows(*out)


def minus_odd_rows(a, b, size):
    out = []
    for i in range(0, C // 2, size):
        out += [a[2 * i : 2 * i + size], a[2 * i + size : 2 * i + 2 * size] - b[i : i + size]]
    return rows(*out)


def iota2(shape, dim):
    return lax.broadcasted_iota(jnp.int32, shape, dim)


def core_index():
    return lax.rem(lax.axis_index("ctx"), 2)


def part(ref, p):
    n, h = divmod(p, HEADS)
    return ref[n * C : n * C + C, h * HD : h * HD + HD]


def maps_kernel(
    k_hbm, v_hbm, ld_hbm, wr_hbm,
    wu_ref, vec_ref, vect_ref, first_ref, keep_ref, send_ref,
    k_ref, v_ref, ld_ref, wr_ref, xs, ts, sems,
):
    copies = [
        pltpu.make_async_copy(src, dst, sems.at[i])
        for i, (src, dst) in enumerate(
            ((ld_hbm, ld_ref), (wr_hbm, wr_ref), (k_hbm, k_ref), (v_hbm, v_ref))
        )
    ]
    for copy in copies:
        copy.start()
    core = core_index()
    row = iota2((C, C), 0)
    col = iota2((C, C), 1)
    eye = row == col
    strict = row > col
    upper = (row <= col).astype(BF16)
    base = row - SUB * lax.div(col, SUB)
    select = lanes(*[(base == j).astype(BF16) for j in range(SUB)])
    for copy in copies[:3]:
        copy.wait()
    steps = rows(ld_ref[:, :C], ld_ref[:, C:])
    beta = rows(wr_ref[:, :C], wr_ref[:, C:])
    s0 = steps.astype(BF16)
    r1 = steps - s0.astype(F32)
    s1 = r1.astype(BF16)
    s2 = (r1 - s1.astype(F32)).astype(BF16)
    g = dot(s0, upper) + (dot(s1, upper) + dot(s2, upper))
    gram = []
    norms = []
    for p in range(NP):
        kp = part(k_ref, p)
        kk = dot_nt(kp, kp)
        gram.append(kk)
        norms.append(jnp.sum(jnp.where(eye, kk, 0.0), axis=0, keepdims=True))
    rn = 1.0 / jnp.sqrt(rows(*norms) + EPS)
    eg = jnp.exp(g)
    gend = g[:, C - 1 : C]
    tail = jnp.exp(gend - g) * rn
    vec = rows(g, beta * rn, tail, rn, eg, beta * eg * rn, beta, beta)
    vec_ref[...] = vec
    vect = rows(vec, vec).T
    vect_ref[...] = vect[:, : NP * 8]

    def column(kind, p):
        i = kind * NP + p
        return vect[:, i : i + 1]

    lower = []
    for p in range(NP):
        spread = column(0, p) - g[p : p + 1, :]
        w = jnp.exp(jnp.where(strict, spread, 0.0))
        w = w * (column(1, p) * rn[p : p + 1, :]) * gram[p]
        lower.append(jnp.where(strict, w, 0.0))
    lane_block = lax.div(iota2((SUB, C), 1), SUB)
    for p in range(NP):
        acc = jnp.zeros((SUB, C), F32)
        for b in range(C // SUB):
            acc = acc + jnp.where(lane_block == b, lower[p][b * SUB : b * SUB + SUB, :], 0.0)
        xs[pl.ds(p, SUB, stride=NP), :] = acc
    xh, xl = split(xs[...])
    coef = dot(lanes(xh, xl), rows(select, select))
    lane_in = lax.rem(iota2((NP, C), 1), SUB)
    solved = []
    for i in range(SUB):
        acc = (lane_in == i).astype(F32)
        for j in range(i):
            acc = acc - coef[i * NP : i * NP + NP, j * C : j * C + C] * solved[j]
        solved.append(acc)
        ts[i * NP : i * NP + NP, :] = acc
    inverse = []
    for p in range(NP):
        tp = ts[pl.ds(p, SUB, stride=NP), :]
        inverse.append(rows(*[jnp.where(lane_block == b, tp, 0.0) for b in range(C // SUB)]))
    system = [split(lower[p]) for p in range(NP)]
    size = SUB
    while size < C:
        mask = lax.div(odd_rows(row, size), size) == lax.div(odd_rows(col, size), size) + 1
        parts = [split(inverse[p]) for p in range(NP)]
        mids = []
        for p in range(NP):
            th, tl = parts[p]
            nh, nl = (odd_rows(a, size) for a in system[p])
            out = dot(lanes(nh, nl), rows(lanes(th, tl), lanes(th, jnp.zeros_like(tl))))
            mids.append(split(jnp.where(mask, out[:, :C] + out[:, C:], 0.0)))
        for p in range(NP):
            th, tl = (odd_rows(a, size) for a in parts[p])
            mh, ml = (at_odd_rows(a, size) for a in mids[p])
            out = dot(lanes(th, tl), rows(lanes(mh, ml), lanes(mh, jnp.zeros_like(ml))))
            inverse[p] = minus_odd_rows(inverse[p], out[:, :C] + out[:, C:], size)
        size *= 2
    copies[3].wait()
    maps = []
    for p in range(NP):
        kp = part(k_ref, p)
        vp = part(v_ref, p)
        eh, el = split(inverse[p] * vec[5 * NP + p : 5 * NP + p + 1, :])
        uh, ul = split(inverse[p] * beta[p : p + 1, :])
        erase = dot(lanes(eh, el), rows(kp, kp))
        write = dot(lanes(uh, ul), rows(vp, vp))
        both = lanes(erase, write)
        wu_ref[p] = rows(*split(both))
        wh, wl = split(both * column(2, p))
        out = dot_tn(rows(kp, kp), rows(wh, wl))
        decay = jnp.where(eye, jnp.exp(gend[p : p + 1, :]), 0.0)
        maps.append(lanes(decay - out[:, :HD], out[:, HD:]))
    whole = []
    for h in range(HEADS):
        first_ref[h] = maps[h]
        whole.append(follow(maps[HEADS + h], maps[h]))
    for h in range(OWN):
        keep_ref[h] = jnp.where(core == 0, whole[h], whole[OWN + h])
        send_ref[h] = jnp.where(core == 0, whole[OWN + h], whole[h]).astype(BF16)


def pair_kernel(keep_ref, recv_ref, total_ref, early_ref):
    core = core_index()
    for h in range(OWN):
        mine = keep_ref[h]
        other = recv_ref[h].astype(F32)
        early = jnp.where(core == 0, mine, other)
        late = jnp.where(core == 0, other, mine)
        early_ref[h] = early
        total_ref[h] = follow(late, early).astype(BF16)


def reads_kernel(q_ref, k_ref, wu_ref, vec_ref, vect_ref, first_ref, qeff_ref, local_ref):
    row = iota2((C, C), 0)
    col = iota2((C, C), 1)
    incl = row >= col
    scale = HD**-0.5
    vec = vec_ref[...]
    vect = vect_ref[...]

    def column(kind, p):
        i = kind * NP + p
        return vect[:, i : i + 1]

    for p in range(NP):
        n, h = divmod(p, HEADS)
        qp = part(q_ref, p)
        qf = qp.astype(F32)
        rq = scale / jnp.sqrt(jnp.sum(qf * qf, axis=1, keepdims=True) + EPS)
        w = jnp.exp(jnp.where(incl, column(0, p) - vec[p : p + 1, :], 0.0))
        scores = w * (rq * vec[3 * NP + p : 3 * NP + p + 1, :]) * dot_nt(qp, part(k_ref, p))
        sh, sl = split(jnp.where(incl, scores, 0.0))
        wh, wl = wu_ref[p, :C], wu_ref[p, C:]
        out = dot(lanes(sh, sl), rows(wh, wh)) + dot(sh, wl)
        qeff = (column(4, p) * rq) * qf - out[:, :HD]
        local = out[:, HD:]
        if n > 0:
            out = dot_wide(qeff, first_ref[h])
            qeff = out[:, :HD]
            local = local + out[:, HD:]
        qeff_ref[h, n * C : n * C + C, :] = qeff.astype(BF16)
        local_ref[h, n * C : n * C + C, :] = local


def y_index():
    return lax.rem(lax.div(lax.axis_index("ctx"), 2), 4)


def x_index():
    return lax.div(lax.axis_index("ctx"), 8)


def follow_sent(later, earlier):
    out = dot(later[:, :HD], earlier)
    return lanes(out[:, :HD], out[:, HD:] + later[:, HD:].astype(F32))


def row_kernel(m_ref, r1_ref, r2_ref, r3_ref, after, total_ref, slots):
    del after
    y = y_index()
    for d, ref in enumerate((m_ref, r1_ref, r2_ref, r3_ref)):
        slots[jnp.bitwise_xor(y, d)] = ref[...]
    for h in range(OWN):
        m0, m1, m2, m3 = (slots[i, h] for i in range(4))
        total_ref[h] = follow(follow_sent(m3, m2), follow_sent(m1, m0)).astype(BF16)


def prefix_kernel(m_ref, r1_ref, r2_ref, r3_ref, early_ref, own_ref, other_ref, slots):
    core = core_index()
    y = y_index()
    for d, ref in enumerate((m_ref, r1_ref, r2_ref, r3_ref)):
        slots[jnp.bitwise_xor(y, d)] = ref[...]
    eye = (iota2((HD, 2 * HD), 0) == iota2((HD, 2 * HD), 1)).astype(F32)
    for h in range(OWN):
        m0, m1, m2 = (slots[i, h] for i in range(3))
        t01 = follow_sent(m1, m0)
        th, tl = split(t01)
        t012 = dot(m2[:, :HD], th) + dot(m2[:, :HD], tl)
        t012 = lanes(t012[:, :HD], t012[:, HD:] + m2[:, HD:].astype(F32))
        first = jnp.where(
            y == 0, eye, jnp.where(y == 1, m0.astype(F32), jnp.where(y == 2, t01, t012))
        )
        second = follow(early_ref[h], first)
        own_ref[h] = jnp.where(core == 0, first, second)
        other_ref[h] = jnp.where(core == 0, second, first)


def state_kernel(m_ref, r1_ref, r2_ref, r3_ref, own_ref, other_ref, keep_ref, send_ref, slots):
    x = x_index()
    for d, ref in enumerate((m_ref, r1_ref, r2_ref, r3_ref)):
        slots[jnp.bitwise_xor(x, d)] = ref[...]
    for h in range(OWN):
        state = jnp.where(x > 0, slots[0, h][:, HD:].astype(F32), 0.0)
        for i in (1, 2):
            m = slots[i, h]
            step = dot_exact_left(m[:, :HD], state) + m[:, HD:].astype(F32)
            state = jnp.where(x > i, step, state)
        own, other = own_ref[h], other_ref[h]
        hi, lo = split(dot_sq(own[:, :HD], state) + own[:, HD:])
        keep_ref[h] = lanes(hi, lo)
        send_ref[h] = (dot_sq(other[:, :HD], state) + other[:, HD:]).astype(BF16)


def gated_rows(state, head, qeff_ref, local_ref, gate_ref, gain):
    out = dot(qeff_ref[head], state)
    core_rows = local_ref[head] + out[:, :HD]
    if state.shape[1] > HD:
        core_rows = core_rows + out[:, HD:]
    mean = jnp.mean(core_rows * core_rows, axis=1, keepdims=True)
    gate = gate_ref[:, pl.ds(pl.multiple_of(head * HD, HD), HD)].astype(F32)
    silu = gate / (1.0 + jnp.exp(-gate))
    return (core_rows / jnp.sqrt(mean + EPS) * gain * silu).astype(BF16)


def gather_rows(state_ref, first, qeff_ref, local_ref, gate_ref, gain_ref, gs, lhs):
    for h in range(OWN):
        gs[:, h * HD : h * HD + HD] = gated_rows(
            state_ref[h], first + h, qeff_ref, local_ref, gate_ref, gain_ref[...]
        )
    me = lax.axis_index("tp")
    chunk = gs.shape[0] // TP
    for d in range(TP):
        start = pl.multiple_of(lax.rem(me + d, TP) * chunk, chunk)
        lhs[d * chunk : d * chunk + chunk, :] = gs[pl.ds(start, chunk), :]


def weight_rows(w_ref, first, s):
    return w_ref[pl.ds(pl.multiple_of(first * HD, OWN * HD), OWN * HD), s]


STEP = 512
ORDER_Y = (1, 2, 3)


def own_kernel(state_ref, qeff_ref, local_ref, gate_ref, gain_ref, w_ref, acc_ref, gs, lhs):
    first = OWN * core_index()
    gather_rows(state_ref, first, qeff_ref, local_ref, gate_ref, gain_ref, gs, lhs)
    for j in range(w_ref.shape[1] // STEP):
        s = slice(j * STEP, j * STEP + STEP)
        acc_ref[:, s] = dot(lhs[...], weight_rows(w_ref, first, s))


def other_kernel(
    state_ref, acc_ref, qeff_ref, local_ref, gate_ref, gain_ref, w_ref, *refs
):
    outs, (gs, lhs) = refs[:-2], refs[-2:]
    first = OWN * (1 - core_index())
    gather_rows(state_ref, first, qeff_ref, local_ref, gate_ref, gain_ref, gs, lhs)
    chunk = gs.shape[0] // TP
    for j in range(w_ref.shape[1] // STEP):
        s = slice(j * STEP, j * STEP + STEP)
        out = (acc_ref[:, s] + dot(lhs[...], weight_rows(w_ref, first, s))).astype(BF16)
        for d, ref in zip((0, 1, 2, 3, 5, 6, 7), outs):
            ref[:, s] = out[d * chunk : d * chunk + chunk]
        ref = outs[7 + j // 2]
        t = slice(j % 2 * STEP, j % 2 * STEP + STEP)
        ref[:, t] = out[4 * chunk : 5 * chunk]


def partial_kernel(a_ref, a3_ref, a4_ref, b_ref, b3_ref, b4_ref, ao_ref, bo_ref):
    half = a4_ref.shape[1]
    a = a_ref[...].astype(F32) + a3_ref[...].astype(F32)
    b = b_ref[...].astype(F32) + b3_ref[...].astype(F32)
    ao_ref[:, :half] = (a[:, :half] + a4_ref[...].astype(F32)).astype(BF16)
    ao_ref[:, half:] = a[:, half:].astype(BF16)
    bo_ref[:, :half] = b[:, :half].astype(BF16)
    bo_ref[:, half:] = (b[:, half:] + b4_ref[...].astype(F32)).astype(BF16)


def sum_kernel(*refs):
    total = refs[0][...].astype(F32)
    for ref in refs[1:-1]:
        total = total + ref[...].astype(F32)
    refs[-1][...] = total.astype(BF16)


def call(kernel, outs, args, scratch=(), hbm=(), flops=10**8, moved=2**20, vmem_mib=32):
    vmem = pl.BlockSpec(memory_space=pltpu.VMEM)
    stay = pl.BlockSpec(memory_space=pltpu.HBM)
    loose = pl.BlockSpec(memory_space=pl.ANY)
    specs = [{"hbm": stay, "any": loose}.get(dict(hbm).get(i), vmem) for i in range(len(args))]
    return pl.pallas_call(
        kernel,
        out_shape=[jax.ShapeDtypeStruct(s, t) for s, t in outs],
        in_specs=specs,
        out_specs=[vmem] * len(outs),
        scratch_shapes=list(scratch),
        compiler_params=pltpu.CompilerParams(vmem_limit_bytes=vmem_mib * 2**20),
        cost_estimate=pl.CostEstimate(flops=flops, bytes_accessed=moved, transcendentals=0),
    )(*args)


def on_device(q, k, v, ld, wr, gate, gain, w):
    tokens = q.shape[0]
    n_ctx = lax.axis_size("ctx")

    def swap(a):
        return lax.ppermute(a, "ctx", [(i, i ^ 1) for i in range(n_ctx)])

    def across_y(a, m):
        pairs = [(i, (i // 8 * 4 + (i // 2 % 4 ^ m)) * 2 + i % 2) for i in range(n_ctx)]
        return lax.ppermute(a, "ctx", pairs)

    def across_x(a, m):
        return lax.ppermute(a, "ctx", [(i, (i // 8 ^ m) * 8 + i % 8) for i in range(n_ctx)])

    def along_z(a, d):
        return lax.ppermute(a, "tp", [(i, (i + d) % TP) for i in range(TP)])

    pair = (OWN, HD, 2 * HD)
    wu, vec, vect, first, keep, send = call(
        maps_kernel,
        [
            ((NP, 2 * C, 2 * HD), BF16),
            ((8 * NP, C), F32),
            ((C, 8 * NP), F32),
            ((HEADS, HD, 2 * HD), F32),
            (pair, F32),
            (pair, BF16),
        ],
        tuple(pltpu.with_memory_space_constraint(a, pltpu.HBM) for a in (k, v, ld, wr)),
        [
            pltpu.VMEM(k.shape, BF16),
            pltpu.VMEM(v.shape, BF16),
            pltpu.VMEM(ld.shape, F32),
            pltpu.VMEM(wr.shape, F32),
            pltpu.VMEM((SUB * NP, C), F32),
            pltpu.VMEM((SUB * NP, C), F32),
            pltpu.SemaphoreType.DMA((4,)),
        ],
        hbm={0: "hbm", 1: "hbm", 2: "hbm", 3: "hbm"},
        flops=10**9,
        vmem_mib=32,
    )
    total, early = call(pair_kernel, [(pair, BF16), (pair, F32)], (keep, swap(send)))
    around = [across_y(total, m) for m in ORDER_Y]
    around = [around[ORDER_Y.index(m)] for m in (1, 2, 3)]
    qeff, local = call(
        reads_kernel,
        [((HEADS, tokens, HD), BF16), ((HEADS, tokens, HD), F32)],
        (q, k, wu, vec, vect, first),
        flops=10**9,
    )
    (row_total,) = call(
        row_kernel,
        [(pair, BF16)],
        (total, *around, local),
        [pltpu.VMEM((4, *pair), BF16)],
        hbm={4: "any"},
    )
    own, other = call(
        prefix_kernel,
        [(pair, F32)] * 2,
        (total, *around, early),
        [pltpu.VMEM((4, *pair), BF16)],
    )
    rows_around = [across_x(row_total, m) for m in (1, 2, 3)]
    own_state, send_state = call(
        state_kernel,
        [(pair, BF16), ((OWN, HD, HD), BF16)],
        (row_total, *rows_around, own, other),
        [pltpu.VMEM((4, *pair), BF16)],
    )
    other_state = swap(send_state)
    gain = gain.reshape(1, HD)
    rows_scratch = [pltpu.VMEM((tokens, OWN * HD), BF16)] * 2
    width = w.shape[1]
    (acc,) = call(
        own_kernel,
        [((tokens, width), F32)],
        (own_state, qeff, local, gate, gain, w),
        rows_scratch,
        flops=10**9,
    )
    rows_here = tokens // TP
    block = ((rows_here, width), BF16)
    p0, p1, p2, p3, p5, p6, p7, p4a, p4b = call(
        other_kernel,
        [block] * 7 + [((rows_here, width // 2), BF16)] * 2,
        (other_state, acc, qeff, local, gate, gain, w),
        rows_scratch,
        flops=10**9,
    )
    a3, b3 = along_z(p3, 1), along_z(p5, -1)
    a4, b4 = along_z(p4a, 2), along_z(p4b, -2)
    a1, b1 = along_z(p1, 1), along_z(p7, -1)
    pa, pb = call(partial_kernel, [block] * 2, (p2, a3, a4, p6, b3, b4))
    a2, b2 = along_z(pa, 2), along_z(pb, -2)
    return call(sum_kernel, [block], (p0, a1, b1, a2, b2))[0]


def solution(mesh):
    in_specs = (
        P("ctx", "tp"),
        P("ctx", "tp"),
        P("ctx", "tp"),
        P("tp", "ctx"),
        P("tp", "ctx"),
        P("ctx", "tp"),
        P(),
        P("tp", None),
    )
    return jax.shard_map(
        on_device, mesh=mesh, in_specs=in_specs, out_specs=P(("ctx", "tp"), None), check_vma=False
    )
```

```python
import jax
import jax.numpy as jnp
from jax import lax
from jax.experimental import pallas as pl
from jax.experimental.pallas import tpu as pltpu
from jax.sharding import PartitionSpec as P

F32 = jnp.float32
BF16 = jnp.bfloat16
EPS = 1e-6
HD = 128
C = 128
HEADS = 4
OWN = 2
NC = 2
NP = HEADS * NC
SUB = 16
TP = 8


def dot(a, b):
    return lax.dot_general(a, b, (((1,), (0,)), ((), ())), preferred_element_type=F32)


def dot_nt(a, b):
    return lax.dot_general(a, b, (((1,), (1,)), ((), ())), preferred_element_type=F32)


def dot_tn(a, b):
    return lax.dot_general(a, b, (((0,), (0,)), ((), ())), preferred_element_type=F32)


def split(a):
    hi = a.astype(BF16)
    lo = (a - hi.astype(F32)).astype(BF16)
    return hi, lo


def lanes(*parts):
    return jnp.concatenate(parts, axis=1)


def rows(*parts):
    return jnp.concatenate(parts, axis=0)


def dot_sq(a, b):
    ah, al = split(a)
    bh, bl = split(b)
    out = dot(lanes(ah, al), rows(lanes(bh, bl), lanes(bh, jnp.zeros_like(bl))))
    return out[:, :C] + out[:, C:]


def dot_wide(a, b):
    ah, al = split(a)
    bh, bl = split(b)
    return dot(lanes(ah, al), rows(bh, bh)) + dot(ah, bl)


def dot_exact_left(a, b):
    bh, bl = split(b)
    out = dot(a, lanes(bh, bl))
    return out[:, :HD] + out[:, HD:]


def follow(later, earlier):
    out = dot_wide(later[:, :HD], earlier)
    return lanes(out[:, :HD], out[:, HD:] + later[:, HD:])


def odd_rows(a, size):
    return rows(*[a[i : i + size] for i in range(size, C, 2 * size)])


def at_odd_rows(a, size):
    zero = jnp.zeros((size, a.shape[1]), a.dtype)
    out = []
    for i in range(0, C // 2, size):
        out += [zero, a[i : i + size]]
    return rows(*out)


def minus_odd_rows(a, b, size):
    out = []
    for i in range(0, C // 2, size):
        out += [a[2 * i : 2 * i + size], a[2 * i + size : 2 * i + 2 * size] - b[i : i + size]]
    return rows(*out)


def iota2(shape, dim):
    return lax.broadcasted_iota(jnp.int32, shape, dim)


def core_index():
    return lax.rem(lax.axis_index("ctx"), 2)


def part(ref, p):
    n, h = divmod(p, HEADS)
    return ref[n * C : n * C + C, h * HD : h * HD + HD]


def maps_kernel(
    k_hbm, v_hbm, ld_hbm, wr_hbm,
    wu_ref, vec_ref, vect_ref, first_ref, keep_ref, send_ref,
    k_ref, v_ref, ld_ref, wr_ref, xs, ts, sems,
):
    copies = [
        pltpu.make_async_copy(src, dst, sems.at[i])
        for i, (src, dst) in enumerate(
            ((ld_hbm, ld_ref), (wr_hbm, wr_ref), (k_hbm, k_ref), (v_hbm, v_ref))
        )
    ]
    for copy in copies:
        copy.start()
    core = core_index()
    row = iota2((C, C), 0)
    col = iota2((C, C), 1)
    eye = row == col
    strict = row > col
    upper = (row <= col).astype(BF16)
    base = row - SUB * lax.div(col, SUB)
    select = lanes(*[(base == j).astype(BF16) for j in range(SUB)])
    for copy in copies[:3]:
        copy.wait()
    steps = rows(ld_ref[:, :C], ld_ref[:, C:])
    beta = rows(wr_ref[:, :C], wr_ref[:, C:])
    s0 = steps.astype(BF16)
    r1 = steps - s0.astype(F32)
    s1 = r1.astype(BF16)
    s2 = (r1 - s1.astype(F32)).astype(BF16)
    g = dot(s0, upper) + (dot(s1, upper) + dot(s2, upper))
    gram = []
    flipped = []
    norms = []
    for p in range(NP):
        kp = part(k_ref, p)
        kt = kp.T
        flipped.append(kt)
        kk = dot(kp, kt)
        gram.append(kk)
        norms.append(jnp.sum(jnp.where(eye, kk, 0.0), axis=0, keepdims=True))
    rn = 1.0 / jnp.sqrt(rows(*norms) + EPS)
    eg = jnp.exp(g)
    gend = g[:, C - 1 : C]
    tail = jnp.exp(gend - g) * rn
    vec = rows(g, beta * rn, tail, rn, eg, beta * eg * rn, beta, beta)
    vec_ref[...] = vec
    vect = rows(vec, vec).T
    vect_ref[...] = vect[:, : NP * 8]

    def column(kind, p):
        i = kind * NP + p
        return vect[:, i : i + 1]

    lower = []
    for p in range(NP):
        spread = column(0, p) - g[p : p + 1, :]
        w = jnp.exp(jnp.where(strict, spread, 0.0))
        w = w * (column(1, p) * rn[p : p + 1, :]) * gram[p]
        lower.append(jnp.where(strict, w, 0.0))
    lane_block = lax.div(iota2((SUB, C), 1), SUB)
    for p in range(NP):
        acc = jnp.zeros((SUB, C), F32)
        for b in range(C // SUB):
            acc = acc + jnp.where(lane_block == b, lower[p][b * SUB : b * SUB + SUB, :], 0.0)
        xs[pl.ds(p, SUB, stride=NP), :] = acc
    xh, xl = split(xs[...])
    coef = dot(lanes(xh, xl), rows(select, select))
    lane_in = lax.rem(iota2((NP, C), 1), SUB)
    solved = []
    for i in range(SUB):
        acc = (lane_in == i).astype(F32)
        for j in range(i):
            acc = acc - coef[i * NP : i * NP + NP, j * C : j * C + C] * solved[j]
        solved.append(acc)
        ts[i * NP : i * NP + NP, :] = acc
    inverse = []
    for p in range(NP):
        tp = ts[pl.ds(p, SUB, stride=NP), :]
        inverse.append(rows(*[jnp.where(lane_block == b, tp, 0.0) for b in range(C // SUB)]))
    system = [split(lower[p]) for p in range(NP)]
    size = SUB
    while size < C:
        mask = lax.div(odd_rows(row, size), size) == lax.div(odd_rows(col, size), size) + 1
        parts = [split(inverse[p]) for p in range(NP)]
        mids = []
        for p in range(NP):
            th, tl = parts[p]
            nh, nl = (odd_rows(a, size) for a in system[p])
            out = dot(rows(nh, nl), th)
            out = out[: C // 2] + out[C // 2 :] + dot(nh, tl)
            mids.append(split(jnp.where(mask, out, 0.0)))
        for p in range(NP):
            th, tl = (odd_rows(a, size) for a in parts[p])
            mh, ml = (at_odd_rows(a, size) for a in mids[p])
            out = dot(rows(th, tl), mh)
            out = out[: C // 2] + out[C // 2 :] + dot(th, ml)
            inverse[p] = minus_odd_rows(inverse[p], out, size)
        size *= 2
    copies[3].wait()
    maps = []
    for p in range(NP):
        kp = part(k_ref, p)
        vp = part(v_ref, p)
        eh, el = split(inverse[p] * vec[5 * NP + p : 5 * NP + p + 1, :])
        uh, ul = split(inverse[p] * beta[p : p + 1, :])
        erase = dot(lanes(eh, el), rows(kp, kp))
        write = dot(lanes(uh, ul), rows(vp, vp))
        both = lanes(erase, write)
        wu_ref[p] = rows(*split(both))
        wh, wl = split(both * column(2, p))
        out = dot(flipped[p], lanes(wh, wl))
        out = out[:, : 2 * HD] + out[:, 2 * HD :]
        decay = jnp.where(eye, jnp.exp(gend[p : p + 1, :]), 0.0)
        maps.append(lanes(decay - out[:, :HD], out[:, HD:]))
    whole = []
    for h in range(HEADS):
        first_ref[h] = maps[h]
        whole.append(follow(maps[HEADS + h], maps[h]))
    for h in range(OWN):
        keep_ref[h] = jnp.where(core == 0, whole[h], whole[OWN + h])
        send_ref[h] = jnp.where(core == 0, whole[OWN + h], whole[h]).astype(BF16)


def pair_kernel(keep_ref, recv_ref, total_ref, early_ref):
    core = core_index()
    for h in range(OWN):
        mine = keep_ref[h]
        other = recv_ref[h].astype(F32)
        early = jnp.where(core == 0, mine, other)
        late = jnp.where(core == 0, other, mine)
        early_ref[h] = early
        total_ref[h] = follow(late, early).astype(BF16)


def reads_kernel(q_ref, k_ref, wu_ref, vec_ref, vect_ref, first_ref, qeff_ref, local_ref):
    row = iota2((C, C), 0)
    col = iota2((C, C), 1)
    incl = row >= col
    scale = HD**-0.5
    vec = vec_ref[...]
    vect = vect_ref[...]

    def column(kind, p):
        i = kind * NP + p
        return vect[:, i : i + 1]

    for p in range(NP):
        n, h = divmod(p, HEADS)
        qp = part(q_ref, p)
        qf = qp.astype(F32)
        rq = scale / jnp.sqrt(jnp.sum(qf * qf, axis=1, keepdims=True) + EPS)
        w = jnp.exp(jnp.where(incl, column(0, p) - vec[p : p + 1, :], 0.0))
        scores = w * (rq * vec[3 * NP + p : 3 * NP + p + 1, :]) * dot_nt(qp, part(k_ref, p))
        sh, sl = split(jnp.where(incl, scores, 0.0))
        wh, wl = wu_ref[p, :C], wu_ref[p, C:]
        out = dot(lanes(sh, sl), rows(wh, wh)) + dot(sh, wl)
        qeff = (column(4, p) * rq) * qf - out[:, :HD]
        local = out[:, HD:]
        if n > 0:
            out = dot_wide(qeff, first_ref[h])
            qeff = out[:, :HD]
            local = local + out[:, HD:]
        qeff_ref[h, n * C : n * C + C, :] = qeff.astype(BF16)
        local_ref[h, n * C : n * C + C, :] = local


def y_index():
    return lax.rem(lax.div(lax.axis_index("ctx"), 2), 4)


def x_index():
    return lax.div(lax.axis_index("ctx"), 8)


def follow_sent(later, earlier):
    out = dot(later[:, :HD], earlier)
    return lanes(out[:, :HD], out[:, HD:] + later[:, HD:].astype(F32))


def row_kernel(m_ref, r1_ref, r2_ref, r3_ref, after, total_ref, slots):
    del after
    y = y_index()
    for d, ref in enumerate((m_ref, r1_ref, r2_ref, r3_ref)):
        slots[jnp.bitwise_xor(y, d)] = ref[...]
    for h in range(OWN):
        m0, m1, m2, m3 = (slots[i, h] for i in range(4))
        total_ref[h] = follow(follow_sent(m3, m2), follow_sent(m1, m0)).astype(BF16)


def prefix_kernel(m_ref, r1_ref, r2_ref, r3_ref, early_ref, own_ref, other_ref, slots):
    core = core_index()
    y = y_index()
    for d, ref in enumerate((m_ref, r1_ref, r2_ref, r3_ref)):
        slots[jnp.bitwise_xor(y, d)] = ref[...]
    eye = (iota2((HD, 2 * HD), 0) == iota2((HD, 2 * HD), 1)).astype(F32)
    for h in range(OWN):
        m0, m1, m2 = (slots[i, h] for i in range(3))
        t01 = follow_sent(m1, m0)
        th, tl = split(t01)
        t012 = dot(m2[:, :HD], th) + dot(m2[:, :HD], tl)
        t012 = lanes(t012[:, :HD], t012[:, HD:] + m2[:, HD:].astype(F32))
        first = jnp.where(
            y == 0, eye, jnp.where(y == 1, m0.astype(F32), jnp.where(y == 2, t01, t012))
        )
        second = follow(early_ref[h], first)
        own_ref[h] = jnp.where(core == 0, first, second)
        other_ref[h] = jnp.where(core == 0, second, first)


def state_kernel(m_ref, r1_ref, r2_ref, r3_ref, own_ref, other_ref, keep_ref, send_ref, slots):
    x = x_index()
    for d, ref in enumerate((m_ref, r1_ref, r2_ref, r3_ref)):
        slots[jnp.bitwise_xor(x, d)] = ref[...]
    for h in range(OWN):
        state = jnp.where(x > 0, slots[0, h][:, HD:].astype(F32), 0.0)
        for i in (1, 2):
            m = slots[i, h]
            step = dot_exact_left(m[:, :HD], state) + m[:, HD:].astype(F32)
            state = jnp.where(x > i, step, state)
        own, other = own_ref[h], other_ref[h]
        hi, lo = split(dot_sq(own[:, :HD], state) + own[:, HD:])
        keep_ref[h] = lanes(hi, lo)
        send_ref[h] = (dot_sq(other[:, :HD], state) + other[:, HD:]).astype(BF16)


def gated_rows(state, head, qeff_ref, local_ref, gate_ref, gain):
    out = dot(qeff_ref[head], state)
    core_rows = local_ref[head] + out[:, :HD]
    if state.shape[1] > HD:
        core_rows = core_rows + out[:, HD:]
    mean = jnp.mean(core_rows * core_rows, axis=1, keepdims=True)
    gate = gate_ref[:, pl.ds(pl.multiple_of(head * HD, HD), HD)].astype(F32)
    silu = gate / (1.0 + jnp.exp(-gate))
    return (core_rows / jnp.sqrt(mean + EPS) * gain * silu).astype(BF16)


def gather_rows(state_ref, first, qeff_ref, local_ref, gate_ref, gain_ref, gs, lhs):
    for h in range(OWN):
        gs[:, h * HD : h * HD + HD] = gated_rows(
            state_ref[h], first + h, qeff_ref, local_ref, gate_ref, gain_ref[...]
        )
    me = lax.axis_index("tp")
    chunk = gs.shape[0] // TP
    for d in range(TP):
        start = pl.multiple_of(lax.rem(me + d, TP) * chunk, chunk)
        lhs[d * chunk : d * chunk + chunk, :] = gs[pl.ds(start, chunk), :]


def weight_rows(w_ref, first, s):
    return w_ref[pl.ds(pl.multiple_of(first * HD, OWN * HD), OWN * HD), s]


STEP = 512
ORDER_Y = (1, 2, 3)


def own_kernel(state_ref, qeff_ref, local_ref, gate_ref, gain_ref, w_ref, acc_ref, gs, lhs):
    first = OWN * core_index()
    gather_rows(state_ref, first, qeff_ref, local_ref, gate_ref, gain_ref, gs, lhs)
    for j in range(w_ref.shape[1] // STEP):
        s = slice(j * STEP, j * STEP + STEP)
        acc_ref[:, s] = dot(lhs[...], weight_rows(w_ref, first, s))


def other_kernel(
    state_ref, acc_ref, qeff_ref, local_ref, gate_ref, gain_ref, w_ref, *refs
):
    outs, (gs, lhs) = refs[:-2], refs[-2:]
    first = OWN * (1 - core_index())
    gather_rows(state_ref, first, qeff_ref, local_ref, gate_ref, gain_ref, gs, lhs)
    chunk = gs.shape[0] // TP
    for j in range(w_ref.shape[1] // STEP):
        s = slice(j * STEP, j * STEP + STEP)
        out = (acc_ref[:, s] + dot(lhs[...], weight_rows(w_ref, first, s))).astype(BF16)
        for d, ref in zip((0, 1, 2, 3, 5, 6, 7), outs):
            ref[:, s] = out[d * chunk : d * chunk + chunk]
        ref = outs[7 + j // 2]
        t = slice(j % 2 * STEP, j % 2 * STEP + STEP)
        ref[:, t] = out[4 * chunk : 5 * chunk]


def partial_kernel(a_ref, a3_ref, a4_ref, b_ref, b3_ref, b4_ref, ao_ref, bo_ref):
    half = a4_ref.shape[1]
    a = a_ref[...].astype(F32) + a3_ref[...].astype(F32)
    b = b_ref[...].astype(F32) + b3_ref[...].astype(F32)
    ao_ref[:, :half] = (a[:, :half] + a4_ref[...].astype(F32)).astype(BF16)
    ao_ref[:, half:] = a[:, half:].astype(BF16)
    bo_ref[:, :half] = b[:, :half].astype(BF16)
    bo_ref[:, half:] = (b[:, half:] + b4_ref[...].astype(F32)).astype(BF16)


def sum_kernel(*refs):
    total = refs[0][...].astype(F32)
    for ref in refs[1:-1]:
        total = total + ref[...].astype(F32)
    refs[-1][...] = total.astype(BF16)


def call(kernel, outs, args, scratch=(), hbm=(), flops=10**8, moved=2**20, vmem_mib=32):
    vmem = pl.BlockSpec(memory_space=pltpu.VMEM)
    stay = pl.BlockSpec(memory_space=pltpu.HBM)
    loose = pl.BlockSpec(memory_space=pl.ANY)
    specs = [{"hbm": stay, "any": loose}.get(dict(hbm).get(i), vmem) for i in range(len(args))]
    return pl.pallas_call(
        kernel,
        out_shape=[jax.ShapeDtypeStruct(s, t) for s, t in outs],
        in_specs=specs,
        out_specs=[vmem] * len(outs),
        scratch_shapes=list(scratch),
        compiler_params=pltpu.CompilerParams(vmem_limit_bytes=vmem_mib * 2**20),
        cost_estimate=pl.CostEstimate(flops=flops, bytes_accessed=moved, transcendentals=0),
    )(*args)


def on_device(q, k, v, ld, wr, gate, gain, w):
    tokens = q.shape[0]
    n_ctx = lax.axis_size("ctx")

    def swap(a):
        return lax.ppermute(a, "ctx", [(i, i ^ 1) for i in range(n_ctx)])

    def across_y(a, m):
        pairs = [(i, (i // 8 * 4 + (i // 2 % 4 ^ m)) * 2 + i % 2) for i in range(n_ctx)]
        return lax.ppermute(a, "ctx", pairs)

    def across_x(a, m):
        return lax.ppermute(a, "ctx", [(i, (i // 8 ^ m) * 8 + i % 8) for i in range(n_ctx)])

    def along_z(a, d):
        return lax.ppermute(a, "tp", [(i, (i + d) % TP) for i in range(TP)])

    pair = (OWN, HD, 2 * HD)
    wu, vec, vect, first, keep, send = call(
        maps_kernel,
        [
            ((NP, 2 * C, 2 * HD), BF16),
            ((8 * NP, C), F32),
            ((C, 8 * NP), F32),
            ((HEADS, HD, 2 * HD), F32),
            (pair, F32),
            (pair, BF16),
        ],
        tuple(pltpu.with_memory_space_constraint(a, pltpu.HBM) for a in (k, v, ld, wr)),
        [
            pltpu.VMEM(k.shape, BF16),
            pltpu.VMEM(v.shape, BF16),
            pltpu.VMEM(ld.shape, F32),
            pltpu.VMEM(wr.shape, F32),
            pltpu.VMEM((SUB * NP, C), F32),
            pltpu.VMEM((SUB * NP, C), F32),
            pltpu.SemaphoreType.DMA((4,)),
        ],
        hbm={0: "hbm", 1: "hbm", 2: "hbm", 3: "hbm"},
        flops=10**9,
        vmem_mib=32,
    )
    total, early = call(pair_kernel, [(pair, BF16), (pair, F32)], (keep, swap(send)))
    around = [across_y(total, m) for m in ORDER_Y]
    around = [around[ORDER_Y.index(m)] for m in (1, 2, 3)]
    qeff, local = call(
        reads_kernel,
        [((HEADS, tokens, HD), BF16), ((HEADS, tokens, HD), F32)],
        (q, k, wu, vec, vect, first),
        flops=10**9,
    )
    (row_total,) = call(
        row_kernel,
        [(pair, BF16)],
        (total, *around, local),
        [pltpu.VMEM((4, *pair), BF16)],
        hbm={4: "any"},
    )
    own, other = call(
        prefix_kernel,
        [(pair, F32)] * 2,
        (total, *around, early),
        [pltpu.VMEM((4, *pair), BF16)],
    )
    rows_around = [across_x(row_total, m) for m in (1, 2, 3)]
    own_state, send_state = call(
        state_kernel,
        [(pair, BF16), ((OWN, HD, HD), BF16)],
        (row_total, *rows_around, own, other),
        [pltpu.VMEM((4, *pair), BF16)],
    )
    other_state = swap(send_state)
    gain = gain.reshape(1, HD)
    rows_scratch = [pltpu.VMEM((tokens, OWN * HD), BF16)] * 2
    width = w.shape[1]
    (acc,) = call(
        own_kernel,
        [((tokens, width), F32)],
        (own_state, qeff, local, gate, gain, w),
        rows_scratch,
        flops=10**9,
    )
    rows_here = tokens // TP
    block = ((rows_here, width), BF16)
    p0, p1, p2, p3, p5, p6, p7, p4a, p4b = call(
        other_kernel,
        [block] * 7 + [((rows_here, width // 2), BF16)] * 2,
        (other_state, acc, qeff, local, gate, gain, w),
        rows_scratch,
        flops=10**9,
    )
    a3, b3 = along_z(p3, 1), along_z(p5, -1)
    a4, b4 = along_z(p4a, 2), along_z(p4b, -2)
    a1, b1 = along_z(p1, 1), along_z(p7, -1)
    pa, pb = call(partial_kernel, [block] * 2, (p2, a3, a4, p6, b3, b4))
    a2, b2 = along_z(pa, 2), along_z(pb, -2)
    return call(sum_kernel, [block], (p0, a1, b1, a2, b2))[0]


def solution(mesh):
    in_specs = (
        P("ctx", "tp"),
        P("ctx", "tp"),
        P("ctx", "tp"),
        P("tp", "ctx"),
        P("tp", "ctx"),
        P("ctx", "tp"),
        P(),
        P("tp", None),
    )
    return jax.shard_map(
        on_device, mesh=mesh, in_specs=in_specs, out_specs=P(("ctx", "tp"), None), check_vma=False
    )
```

```python
import jax
import jax.numpy as jnp
from jax import lax
from jax.experimental import pallas as pl
from jax.experimental.pallas import tpu as pltpu
from jax.sharding import PartitionSpec as P

F32 = jnp.float32
BF16 = jnp.bfloat16
EPS = 1e-6
HD = 128
C = 128
HEADS = 4
OWN = 2
NC = 2
NP = HEADS * NC
SUB = 16
TP = 8


def dot(a, b):
    return lax.dot_general(a, b, (((1,), (0,)), ((), ())), preferred_element_type=F32)


def dot_nt(a, b):
    return lax.dot_general(a, b, (((1,), (1,)), ((), ())), preferred_element_type=F32)


def dot_tn(a, b):
    return lax.dot_general(a, b, (((0,), (0,)), ((), ())), preferred_element_type=F32)


def split(a):
    hi = a.astype(BF16)
    lo = (a - hi.astype(F32)).astype(BF16)
    return hi, lo


def lanes(*parts):
    return jnp.concatenate(parts, axis=1)


def rows(*parts):
    return jnp.concatenate(parts, axis=0)


def dot_sq(a, b):
    ah, al = split(a)
    bh, bl = split(b)
    out = dot(lanes(ah, al), rows(lanes(bh, bl), lanes(bh, jnp.zeros_like(bl))))
    return out[:, :C] + out[:, C:]


def dot_wide(a, b):
    ah, al = split(a)
    bh, bl = split(b)
    return dot(lanes(ah, al), rows(bh, bh)) + dot(ah, bl)


def dot_exact_left(a, b):
    bh, bl = split(b)
    out = dot(a, lanes(bh, bl))
    return out[:, :HD] + out[:, HD:]


def follow(later, earlier):
    out = dot_wide(later[:, :HD], earlier)
    return lanes(out[:, :HD], out[:, HD:] + later[:, HD:])


def odd_rows(a, size):
    return rows(*[a[i : i + size] for i in range(size, C, 2 * size)])


def at_odd_rows(a, size):
    zero = jnp.zeros((size, a.shape[1]), a.dtype)
    out = []
    for i in range(0, C // 2, size):
        out += [zero, a[i : i + size]]
    return rows(*out)


def minus_odd_rows(a, b, size):
    out = []
    for i in range(0, C // 2, size):
        out += [a[2 * i : 2 * i + size], a[2 * i + size : 2 * i + 2 * size] - b[i : i + size]]
    return rows(*out)


def iota2(shape, dim):
    return lax.broadcasted_iota(jnp.int32, shape, dim)


def core_index():
    return lax.rem(lax.axis_index("ctx"), 2)


def part(ref, p):
    n, h = divmod(p, HEADS)
    return ref[n * C : n * C + C, h * HD : h * HD + HD]


def maps_kernel(
    k_hbm, v_hbm, ld_hbm, wr_hbm,
    wu_ref, vec_ref, vect_ref, first_ref, keep_ref, send_ref,
    k_ref, v_ref, ld_ref, wr_ref, xs, ts, sems,
):
    copies = [
        pltpu.make_async_copy(src, dst, sems.at[i])
        for i, (src, dst) in enumerate(
            ((ld_hbm, ld_ref), (wr_hbm, wr_ref), (k_hbm, k_ref), (v_hbm, v_ref))
        )
    ]
    for copy in copies:
        copy.start()
    core = core_index()
    row = iota2((C, C), 0)
    col = iota2((C, C), 1)
    eye = row == col
    strict = row > col
    upper = (row <= col).astype(BF16)
    base = row - SUB * lax.div(col, SUB)
    select = lanes(*[(base == j).astype(BF16) for j in range(SUB)])
    for copy in copies[:3]:
        copy.wait()
    steps = rows(ld_ref[:, :C], ld_ref[:, C:])
    beta = rows(wr_ref[:, :C], wr_ref[:, C:])
    s0 = steps.astype(BF16)
    r1 = steps - s0.astype(F32)
    s1 = r1.astype(BF16)
    s2 = (r1 - s1.astype(F32)).astype(BF16)
    g = dot(s0, upper) + (dot(s1, upper) + dot(s2, upper))
    gram = []
    flipped = []
    norms = []
    for p in range(NP):
        kp = part(k_ref, p)
        kt = kp.T
        flipped.append(kt)
        kk = dot(kp, kt)
        gram.append(kk)
        kf = kt.astype(F32)
        norms.append(jnp.sum(kf * kf, axis=0, keepdims=True))
    rn = 1.0 / jnp.sqrt(rows(*norms) + EPS)
    eg = jnp.exp(g)
    gend = g[:, C - 1 : C]
    tail = jnp.exp(gend - g) * rn
    vec = rows(g, beta * rn, tail, rn, eg, beta * eg * rn, beta, beta)
    vec_ref[...] = vec
    vect = rows(vec, vec).T
    vect_ref[...] = vect[:, : NP * 8]

    def column(kind, p):
        i = kind * NP + p
        return vect[:, i : i + 1]

    lower = []
    for p in range(NP):
        spread = column(0, p) - g[p : p + 1, :]
        w = jnp.exp(jnp.where(strict, spread, 0.0))
        w = w * (column(1, p) * rn[p : p + 1, :]) * gram[p]
        lower.append(jnp.where(strict, w, 0.0))
    lane_block = lax.div(iota2((SUB, C), 1), SUB)
    for p in range(NP):
        acc = jnp.zeros((SUB, C), F32)
        for b in range(C // SUB):
            acc = acc + jnp.where(lane_block == b, lower[p][b * SUB : b * SUB + SUB, :], 0.0)
        xs[pl.ds(p, SUB, stride=NP), :] = acc
    xh, xl = split(xs[...])
    coef = dot(lanes(xh, xl), rows(select, select))
    lane_in = lax.rem(iota2((NP, C), 1), SUB)
    solved = []
    for i in range(SUB):
        acc = (lane_in == i).astype(F32)
        for j in range(i):
            acc = acc - coef[i * NP : i * NP + NP, j * C : j * C + C] * solved[j]
        solved.append(acc)
        ts[i * NP : i * NP + NP, :] = acc
    inverse = []
    for p in range(NP):
        tp = ts[pl.ds(p, SUB, stride=NP), :]
        inverse.append(rows(*[jnp.where(lane_block == b, tp, 0.0) for b in range(C // SUB)]))
    system = [split(lower[p]) for p in range(NP)]
    size = SUB
    while size < C:
        mask = lax.div(odd_rows(row, size), size) == lax.div(odd_rows(col, size), size) + 1
        parts = [split(inverse[p]) for p in range(NP)]
        mids = []
        for p in range(NP):
            th, tl = parts[p]
            nh, nl = (odd_rows(a, size) for a in system[p])
            out = dot(rows(nh, nl), th)
            out = out[: C // 2] + out[C // 2 :] + dot(nh, tl)
            mids.append(split(jnp.where(mask, out, 0.0)))
        for p in range(NP):
            th, tl = (odd_rows(a, size) for a in parts[p])
            mh, ml = (at_odd_rows(a, size) for a in mids[p])
            out = dot(rows(th, tl), mh)
            out = out[: C // 2] + out[C // 2 :] + dot(th, ml)
            inverse[p] = minus_odd_rows(inverse[p], out, size)
        size *= 2
    copies[3].wait()
    maps = []
    for p in range(NP):
        kp = part(k_ref, p)
        vp = part(v_ref, p)
        eh, el = split(inverse[p] * vec[5 * NP + p : 5 * NP + p + 1, :])
        uh, ul = split(inverse[p] * beta[p : p + 1, :])
        erase = dot(lanes(eh, el), rows(kp, kp))
        write = dot(lanes(uh, ul), rows(vp, vp))
        both = lanes(erase, write)
        wu_ref[p] = rows(*split(both))
        wh, wl = split(both * column(2, p))
        out = dot(flipped[p], lanes(wh, wl))
        out = out[:, : 2 * HD] + out[:, 2 * HD :]
        decay = jnp.where(eye, jnp.exp(gend[p : p + 1, :]), 0.0)
        maps.append(lanes(decay - out[:, :HD], out[:, HD:]))
    whole = []
    for h in range(HEADS):
        first_ref[h] = maps[h]
        whole.append(follow(maps[HEADS + h], maps[h]))
    for h in range(OWN):
        keep_ref[h] = jnp.where(core == 0, whole[h], whole[OWN + h])
        send_ref[h] = jnp.where(core == 0, whole[OWN + h], whole[h]).astype(BF16)


def pair_kernel(keep_ref, recv_ref, *refs):
    *total_refs, early_ref = refs
    core = core_index()
    for h in range(OWN):
        mine = keep_ref[h]
        other = recv_ref[h].astype(F32)
        early = jnp.where(core == 0, mine, other)
        late = jnp.where(core == 0, other, mine)
        early_ref[h] = early
        total = follow(late, early).astype(BF16)
        for ref in total_refs:
            ref[h] = total


def reads_kernel(
    q_ref, k_ref, wu_ref, vec_ref, vect_ref, first_ref, gate_ref, gain_ref,
    qeff_ref, local_ref, factor_ref,
):
    row = iota2((C, C), 0)
    col = iota2((C, C), 1)
    incl = row >= col
    scale = HD**-0.5
    vec = vec_ref[...]
    vect = vect_ref[...]

    def column(kind, p):
        i = kind * NP + p
        return vect[:, i : i + 1]

    for h in range(HEADS):
        gate = gate_ref[:, h * HD : h * HD + HD].astype(F32)
        factor_ref[h] = gain_ref[...] * (gate / (1.0 + jnp.exp(-gate)))
    for p in range(NP):
        n, h = divmod(p, HEADS)
        qp = part(q_ref, p)
        qf = qp.astype(F32)
        rq = scale / jnp.sqrt(jnp.sum(qf * qf, axis=1, keepdims=True) + EPS)
        w = jnp.exp(jnp.where(incl, column(0, p) - vec[p : p + 1, :], 0.0))
        scores = w * (rq * vec[3 * NP + p : 3 * NP + p + 1, :]) * dot_nt(qp, part(k_ref, p))
        sh, sl = split(jnp.where(incl, scores, 0.0))
        wh, wl = wu_ref[p, :C], wu_ref[p, C:]
        out = dot(lanes(sh, sl), rows(wh, wh)) + dot(sh, wl)
        qeff = (column(4, p) * rq) * qf - out[:, :HD]
        local = out[:, HD:]
        if n > 0:
            out = dot_wide(qeff, first_ref[h])
            qeff = out[:, :HD]
            local = local + out[:, HD:]
        qeff_ref[h, n * C : n * C + C, :] = qeff.astype(BF16)
        local_ref[h, n * C : n * C + C, :] = local


def y_index():
    return lax.rem(lax.div(lax.axis_index("ctx"), 2), 4)


def x_index():
    return lax.div(lax.axis_index("ctx"), 8)


def follow_sent(later, earlier):
    out = dot(later[:, :HD], earlier)
    return lanes(out[:, :HD], out[:, HD:] + later[:, HD:].astype(F32))


def row_kernel(m_ref, r1_ref, r2_ref, r3_ref, after, *refs):
    del after
    *total_refs, slots = refs
    y = y_index()
    for d, ref in enumerate((m_ref, r1_ref, r2_ref, r3_ref)):
        slots[jnp.bitwise_xor(y, d)] = ref[...]
    for h in range(OWN):
        m0, m1, m2, m3 = (slots[i, h] for i in range(4))
        total = follow(follow_sent(m3, m2), follow_sent(m1, m0)).astype(BF16)
        for ref in total_refs:
            ref[h] = total


def prefix_kernel(m_ref, r1_ref, r2_ref, r3_ref, early_ref, own_ref, other_ref, slots):
    core = core_index()
    y = y_index()
    for d, ref in enumerate((m_ref, r1_ref, r2_ref, r3_ref)):
        slots[jnp.bitwise_xor(y, d)] = ref[...]
    eye = (iota2((HD, 2 * HD), 0) == iota2((HD, 2 * HD), 1)).astype(F32)
    for h in range(OWN):
        m0, m1, m2 = (slots[i, h] for i in range(3))
        t01 = follow_sent(m1, m0)
        th, tl = split(t01)
        t012 = dot(m2[:, :HD], th) + dot(m2[:, :HD], tl)
        t012 = lanes(t012[:, :HD], t012[:, HD:] + m2[:, HD:].astype(F32))
        first = jnp.where(
            y == 0, eye, jnp.where(y == 1, m0.astype(F32), jnp.where(y == 2, t01, t012))
        )
        second = follow(early_ref[h], first)
        own_ref[h] = jnp.where(core == 0, first, second)
        other_ref[h] = jnp.where(core == 0, second, first)


def state_kernel(m_ref, r1_ref, r2_ref, r3_ref, own_ref, other_ref, keep_ref, send_ref, slots):
    x = x_index()
    for d, ref in enumerate((m_ref, r1_ref, r2_ref, r3_ref)):
        slots[jnp.bitwise_xor(x, d)] = ref[...]
    for h in range(OWN):
        state = jnp.where(x > 0, slots[0, h][:, HD:].astype(F32), 0.0)
        for i in (1, 2):
            m = slots[i, h]
            step = dot_exact_left(m[:, :HD], state) + m[:, HD:].astype(F32)
            state = jnp.where(x > i, step, state)
        own, other = own_ref[h], other_ref[h]
        hi, lo = split(dot_sq(own[:, :HD], state) + own[:, HD:])
        keep_ref[h] = lanes(hi, lo)
        send_ref[h] = (dot_sq(other[:, :HD], state) + other[:, HD:]).astype(BF16)


def gated_rows(state, head, qeff_ref, local_ref, factor_ref):
    out = dot(qeff_ref[head], state)
    core_rows = local_ref[head] + out[:, :HD]
    if state.shape[1] > HD:
        core_rows = core_rows + out[:, HD:]
    mean = jnp.mean(core_rows * core_rows, axis=1, keepdims=True)
    return (core_rows * (1.0 / jnp.sqrt(mean + EPS)) * factor_ref[head]).astype(BF16)


def gather_rows(state_ref, first, qeff_ref, local_ref, factor_ref, gs, lhs):
    for h in range(OWN):
        gs[:, h * HD : h * HD + HD] = gated_rows(
            state_ref[h], first + h, qeff_ref, local_ref, factor_ref
        )
    me = lax.axis_index("tp")
    chunk = gs.shape[0] // TP
    for d in range(TP):
        start = pl.multiple_of(lax.rem(me + d, TP) * chunk, chunk)
        lhs[d * chunk : d * chunk + chunk, :] = gs[pl.ds(start, chunk), :]


def weight_rows(w_ref, first, s):
    return w_ref[pl.ds(pl.multiple_of(first * HD, OWN * HD), OWN * HD), s]


STEP = 512
ORDER_Y = (1, 2, 3)
ORDER_X = (1, 2, 3)


def own_kernel(state_ref, qeff_ref, local_ref, factor_ref, w_ref, acc_ref, gs, lhs):
    first = OWN * core_index()
    gather_rows(state_ref, first, qeff_ref, local_ref, factor_ref, gs, lhs)
    for j in range(w_ref.shape[1] // STEP):
        s = slice(j * STEP, j * STEP + STEP)
        acc_ref[:, s] = dot(lhs[...], weight_rows(w_ref, first, s))


def other_kernel(state_ref, acc_ref, qeff_ref, local_ref, factor_ref, w_ref, *refs):
    outs, (gs, lhs) = refs[:-2], refs[-2:]
    first = OWN * (1 - core_index())
    gather_rows(state_ref, first, qeff_ref, local_ref, factor_ref, gs, lhs)
    chunk = gs.shape[0] // TP
    for j in range(w_ref.shape[1] // STEP):
        s = slice(j * STEP, j * STEP + STEP)
        out = (acc_ref[:, s] + dot(lhs[...], weight_rows(w_ref, first, s))).astype(BF16)
        for d, ref in zip((0, 1, 2, 3, 5, 6, 7), outs):
            ref[:, s] = out[d * chunk : d * chunk + chunk]
        ref = outs[7 + j // 2]
        t = slice(j % 2 * STEP, j % 2 * STEP + STEP)
        ref[:, t] = out[4 * chunk : 5 * chunk]


def partial_kernel(a_ref, a3_ref, a4_ref, b_ref, b3_ref, b4_ref, ao_ref, bo_ref):
    half = a4_ref.shape[1]
    a = a_ref[...].astype(F32) + a3_ref[...].astype(F32)
    b = b_ref[...].astype(F32) + b3_ref[...].astype(F32)
    ao_ref[:, :half] = (a[:, :half] + a4_ref[...].astype(F32)).astype(BF16)
    ao_ref[:, half:] = a[:, half:].astype(BF16)
    bo_ref[:, :half] = b[:, :half].astype(BF16)
    bo_ref[:, half:] = (b[:, half:] + b4_ref[...].astype(F32)).astype(BF16)


def sum_kernel(*refs):
    total = refs[0][...].astype(F32)
    for ref in refs[1:-1]:
        total = total + ref[...].astype(F32)
    refs[-1][...] = total.astype(BF16)


def call(kernel, outs, args, scratch=(), hbm=(), flops=10**8, moved=2**20, vmem_mib=32):
    vmem = pl.BlockSpec(memory_space=pltpu.VMEM)
    stay = pl.BlockSpec(memory_space=pltpu.HBM)
    loose = pl.BlockSpec(memory_space=pl.ANY)
    specs = [{"hbm": stay, "any": loose}.get(dict(hbm).get(i), vmem) for i in range(len(args))]
    return pl.pallas_call(
        kernel,
        out_shape=[jax.ShapeDtypeStruct(s, t) for s, t in outs],
        in_specs=specs,
        out_specs=[vmem] * len(outs),
        scratch_shapes=list(scratch),
        compiler_params=pltpu.CompilerParams(vmem_limit_bytes=vmem_mib * 2**20),
        cost_estimate=pl.CostEstimate(flops=flops, bytes_accessed=moved, transcendentals=0),
    )(*args)


def on_device(q, k, v, ld, wr, gate, gain, w):
    tokens = q.shape[0]
    n_ctx = lax.axis_size("ctx")

    def swap(a):
        return lax.ppermute(a, "ctx", [(i, i ^ 1) for i in range(n_ctx)])

    def across_y(a, m):
        pairs = [(i, (i // 8 * 4 + (i // 2 % 4 ^ m)) * 2 + i % 2) for i in range(n_ctx)]
        return lax.ppermute(a, "ctx", pairs)

    def across_x(a, m):
        return lax.ppermute(a, "ctx", [(i, (i // 8 ^ m) * 8 + i % 8) for i in range(n_ctx)])

    def along_z(a, d):
        return lax.ppermute(a, "tp", [(i, (i + d) % TP) for i in range(TP)])

    pair = (OWN, HD, 2 * HD)
    wu, vec, vect, first, keep, send = call(
        maps_kernel,
        [
            ((NP, 2 * C, 2 * HD), BF16),
            ((8 * NP, C), F32),
            ((C, 8 * NP), F32),
            ((HEADS, HD, 2 * HD), F32),
            (pair, F32),
            (pair, BF16),
        ],
        tuple(pltpu.with_memory_space_constraint(a, pltpu.HBM) for a in (k, v, ld, wr)),
        [
            pltpu.VMEM(k.shape, BF16),
            pltpu.VMEM(v.shape, BF16),
            pltpu.VMEM(ld.shape, F32),
            pltpu.VMEM(wr.shape, F32),
            pltpu.VMEM((SUB * NP, C), F32),
            pltpu.VMEM((SUB * NP, C), F32),
            pltpu.SemaphoreType.DMA((4,)),
        ],
        hbm={0: "hbm", 1: "hbm", 2: "hbm", 3: "hbm"},
        flops=10**9,
        vmem_mib=32,
    )
    *totals, early = call(pair_kernel, [(pair, BF16)] * 3 + [(pair, F32)], (keep, swap(send)))
    total = totals[0]
    around = [across_y(totals[ORDER_Y.index(m)], m) for m in (1, 2, 3)]
    qeff, local, factor = call(
        reads_kernel,
        [((HEADS, tokens, HD), BF16)] + [((HEADS, tokens, HD), F32)] * 2,
        (q, k, wu, vec, vect, first, gate, gain.reshape(1, HD)),
        flops=10**9,
    )
    row_totals = call(
        row_kernel,
        [(pair, BF16)] * 3,
        (total, *around, local),
        [pltpu.VMEM((4, *pair), BF16)],
        hbm={4: "any"},
    )
    own, other = call(
        prefix_kernel,
        [(pair, F32)] * 2,
        (total, *around, early),
        [pltpu.VMEM((4, *pair), BF16)],
    )
    rows_around = [across_x(row_totals[ORDER_X.index(m)], m) for m in (1, 2, 3)]
    own_state, send_state = call(
        state_kernel,
        [(pair, BF16), ((OWN, HD, HD), BF16)],
        (row_totals[0], *rows_around, own, other),
        [pltpu.VMEM((4, *pair), BF16)],
    )
    other_state = swap(send_state)
    rows_scratch = [pltpu.VMEM((tokens, OWN * HD), BF16)] * 2
    width = w.shape[1]
    (acc,) = call(
        own_kernel,
        [((tokens, width), F32)],
        (own_state, qeff, local, factor, w),
        rows_scratch,
        flops=10**9,
    )
    rows_here = tokens // TP
    block = ((rows_here, width), BF16)
    p0, p1, p2, p3, p5, p6, p7, p4a, p4b = call(
        other_kernel,
        [block] * 7 + [((rows_here, width // 2), BF16)] * 2,
        (other_state, acc, qeff, local, factor, w),
        rows_scratch,
        flops=10**9,
    )
    a3, b3 = along_z(p3, 1), along_z(p5, -1)
    a4, b4 = along_z(p4a, 2), along_z(p4b, -2)
    a1, b1 = along_z(p1, 1), along_z(p7, -1)
    pa, pb = call(partial_kernel, [block] * 2, (p2, a3, a4, p6, b3, b4))
    a2, b2 = along_z(pa, 2), along_z(pb, -2)
    return call(sum_kernel, [block], (p0, a1, b1, a2, b2))[0]


def solution(mesh):
    in_specs = (
        P("ctx", "tp"),
        P("ctx", "tp"),
        P("ctx", "tp"),
        P("tp", "ctx"),
        P("tp", "ctx"),
        P("ctx", "tp"),
        P(),
        P("tp", None),
    )
    return jax.shard_map(
        on_device, mesh=mesh, in_specs=in_specs, out_specs=P(("ctx", "tp"), None), check_vma=False
    )
```

```python
import jax
import jax.numpy as jnp
from jax import lax
from jax.experimental import pallas as pl
from jax.experimental.pallas import tpu as pltpu
from jax.sharding import PartitionSpec as P

F32 = jnp.float32
BF16 = jnp.bfloat16
EPS = 1e-6
HD = 128
C = 128
HEADS = 4
OWN = 2
NC = 2
NP = HEADS * NC
SUB = 16
TP = 8


def dot(a, b):
    return lax.dot_general(a, b, (((1,), (0,)), ((), ())), preferred_element_type=F32)


def dot_nt(a, b):
    return lax.dot_general(a, b, (((1,), (1,)), ((), ())), preferred_element_type=F32)


def dot_tn(a, b):
    return lax.dot_general(a, b, (((0,), (0,)), ((), ())), preferred_element_type=F32)


def split(a):
    hi = a.astype(BF16)
    lo = (a - hi.astype(F32)).astype(BF16)
    return hi, lo


def lanes(*parts):
    return jnp.concatenate(parts, axis=1)


def rows(*parts):
    return jnp.concatenate(parts, axis=0)


def dot_sq(a, b):
    ah, al = split(a)
    bh, bl = split(b)
    out = dot(lanes(ah, al), rows(lanes(bh, bl), lanes(bh, jnp.zeros_like(bl))))
    return out[:, :C] + out[:, C:]


def dot_wide(a, b):
    ah, al = split(a)
    bh, bl = split(b)
    return dot(lanes(ah, al), rows(bh, bh)) + dot(ah, bl)


def dot_exact_left(a, b):
    bh, bl = split(b)
    out = dot(a, lanes(bh, bl))
    return out[:, :HD] + out[:, HD:]


def follow(later, earlier):
    out = dot_wide(later[:, :HD], earlier)
    return lanes(out[:, :HD], out[:, HD:] + later[:, HD:])


def odd_rows(a, size):
    return rows(*[a[i : i + size] for i in range(size, C, 2 * size)])


def at_odd_rows(a, size):
    zero = jnp.zeros((size, a.shape[1]), a.dtype)
    out = []
    for i in range(0, C // 2, size):
        out += [zero, a[i : i + size]]
    return rows(*out)


def minus_odd_rows(a, b, size):
    out = []
    for i in range(0, C // 2, size):
        out += [a[2 * i : 2 * i + size], a[2 * i + size : 2 * i + 2 * size] - b[i : i + size]]
    return rows(*out)


def iota2(shape, dim):
    return lax.broadcasted_iota(jnp.int32, shape, dim)


def core_index():
    return lax.rem(lax.axis_index("ctx"), 2)


def part(ref, p):
    n, h = divmod(p, HEADS)
    return ref[n * C : n * C + C, h * HD : h * HD + HD]


def maps_kernel(
    k_hbm, v_hbm, ld_hbm, wr_hbm,
    wu_ref, vec_ref, vect_ref, first_ref, keep_ref, send_ref,
    k_ref, v_ref, ld_ref, wr_ref, xs, ts, sems,
):
    copies = [
        pltpu.make_async_copy(src, dst, sems.at[i])
        for i, (src, dst) in enumerate(
            ((ld_hbm, ld_ref), (wr_hbm, wr_ref), (k_hbm, k_ref), (v_hbm, v_ref))
        )
    ]
    for copy in copies:
        copy.start()
    core = core_index()
    row = iota2((C, C), 0)
    col = iota2((C, C), 1)
    eye = row == col
    strict = row > col
    upper = (row <= col).astype(BF16)
    base = row - SUB * lax.div(col, SUB)
    select = lanes(*[(base == j).astype(BF16) for j in range(SUB)])
    for copy in copies[:3]:
        copy.wait()
    steps = rows(ld_ref[:, :C], ld_ref[:, C:])
    beta = rows(wr_ref[:, :C], wr_ref[:, C:])
    s0 = steps.astype(BF16)
    r1 = steps - s0.astype(F32)
    s1 = r1.astype(BF16)
    s2 = (r1 - s1.astype(F32)).astype(BF16)
    g = dot(s0, upper) + (dot(s1, upper) + dot(s2, upper))
    gram = []
    flipped = []
    norms = []
    for p in range(NP):
        kp = part(k_ref, p)
        kt = kp.T
        flipped.append(kt)
        kk = dot(kp, kt)
        gram.append(kk)
        kf = kt.astype(F32)
        norms.append(jnp.sum(kf * kf, axis=0, keepdims=True))
    rn = 1.0 / jnp.sqrt(rows(*norms) + EPS)
    eg = jnp.exp(g)
    gend = g[:, C - 1 : C]
    tail = jnp.exp(gend - g) * rn
    vec = rows(g, beta * rn, tail, rn, eg, beta * eg * rn, beta, beta)
    vec_ref[...] = vec
    vect = rows(vec, vec).T
    vect_ref[...] = vect[:, : NP * 8]

    def column(kind, p):
        i = kind * NP + p
        return vect[:, i : i + 1]

    lower = []
    for p in range(NP):
        spread = column(0, p) - g[p : p + 1, :]
        w = jnp.exp(jnp.where(strict, spread, 0.0))
        w = w * (column(1, p) * rn[p : p + 1, :]) * gram[p]
        lower.append(jnp.where(strict, w, 0.0))
    lane_block = lax.div(iota2((SUB, C), 1), SUB)
    for p in range(NP):
        acc = jnp.zeros((SUB, C), F32)
        for b in range(C // SUB):
            acc = acc + jnp.where(lane_block == b, lower[p][b * SUB : b * SUB + SUB, :], 0.0)
        xs[pl.ds(p, SUB, stride=NP), :] = acc
    xh, xl = split(xs[...])
    coef = dot(lanes(xh, xl), rows(select, select))
    lane_in = lax.rem(iota2((NP, C), 1), SUB)
    solved = []
    for i in range(SUB):
        acc = (lane_in == i).astype(F32)
        for j in range(i):
            acc = acc - coef[i * NP : i * NP + NP, j * C : j * C + C] * solved[j]
        solved.append(acc)
        ts[i * NP : i * NP + NP, :] = acc
    inverse = []
    for p in range(NP):
        tp = ts[pl.ds(p, SUB, stride=NP), :]
        inverse.append(rows(*[jnp.where(lane_block == b, tp, 0.0) for b in range(C // SUB)]))
    system = [split(lower[p]) for p in range(NP)]
    size = SUB
    while size < C:
        mask = lax.div(odd_rows(row, size), size) == lax.div(odd_rows(col, size), size) + 1
        parts = [split(inverse[p]) for p in range(NP)]
        mids = []
        for p in range(NP):
            th, tl = parts[p]
            nh, nl = (odd_rows(a, size) for a in system[p])
            out = dot(rows(nh, nl), th)
            out = out[: C // 2] + out[C // 2 :] + dot(nh, tl)
            mids.append(split(jnp.where(mask, out, 0.0)))
        for p in range(NP):
            th, tl = (odd_rows(a, size) for a in parts[p])
            mh, ml = (at_odd_rows(a, size) for a in mids[p])
            out = dot(rows(th, tl), mh)
            out = out[: C // 2] + out[C // 2 :] + dot(th, ml)
            inverse[p] = minus_odd_rows(inverse[p], out, size)
        size *= 2
    copies[3].wait()
    maps = []
    for p in range(NP):
        kp = part(k_ref, p)
        vp = part(v_ref, p)
        eh, el = split(inverse[p] * vec[5 * NP + p : 5 * NP + p + 1, :])
        uh, ul = split(inverse[p] * beta[p : p + 1, :])
        erase = dot(lanes(eh, el), rows(kp, kp))
        write = dot(lanes(uh, ul), rows(vp, vp))
        both = lanes(erase, write)
        wu_ref[p] = rows(*split(both))
        wh, wl = split(both * column(2, p))
        out = dot(flipped[p], lanes(wh, wl))
        out = out[:, : 2 * HD] + out[:, 2 * HD :]
        decay = jnp.where(eye, jnp.exp(gend[p : p + 1, :]), 0.0)
        maps.append(lanes(decay - out[:, :HD], out[:, HD:]))
    whole = []
    for h in range(HEADS):
        first_ref[h] = maps[h]
        whole.append(follow(maps[HEADS + h], maps[h]))
    for h in range(OWN):
        keep_ref[h] = jnp.where(core == 0, whole[h], whole[OWN + h])
        send_ref[h] = jnp.where(core == 0, whole[OWN + h], whole[h]).astype(BF16)


def pair_kernel(keep_ref, recv_ref, *refs):
    *total_refs, early_ref = refs
    core = core_index()
    for h in range(OWN):
        mine = keep_ref[h]
        other = recv_ref[h].astype(F32)
        early = jnp.where(core == 0, mine, other)
        late = jnp.where(core == 0, other, mine)
        early_ref[h] = early
        total = follow(late, early).astype(BF16)
        for ref in total_refs:
            ref[h] = total


def reads_kernel(
    q_ref, k_ref, wu_ref, vec_ref, vect_ref, first_ref, gate_ref, gain_ref,
    qeff_ref, local_ref, factor_ref,
):
    row = iota2((C, C), 0)
    col = iota2((C, C), 1)
    incl = row >= col
    scale = HD**-0.5
    vec = vec_ref[...]
    vect = vect_ref[...]

    def column(kind, p):
        i = kind * NP + p
        return vect[:, i : i + 1]

    for h in range(HEADS):
        gate = gate_ref[:, h * HD : h * HD + HD].astype(F32)
        factor_ref[h] = gain_ref[...] * (gate / (1.0 + jnp.exp(-gate)))
    for p in range(NP):
        n, h = divmod(p, HEADS)
        qp = part(q_ref, p)
        qf = qp.astype(F32)
        rq = scale / jnp.sqrt(jnp.sum(qf * qf, axis=1, keepdims=True) + EPS)
        w = jnp.exp(jnp.where(incl, column(0, p) - vec[p : p + 1, :], 0.0))
        scores = w * (rq * vec[3 * NP + p : 3 * NP + p + 1, :]) * dot_nt(qp, part(k_ref, p))
        sh, sl = split(jnp.where(incl, scores, 0.0))
        wh, wl = wu_ref[p, :C], wu_ref[p, C:]
        out = dot(lanes(sh, sl), rows(wh, wh)) + dot(sh, wl)
        qeff = (column(4, p) * rq) * qf - out[:, :HD]
        local = out[:, HD:]
        if n > 0:
            out = dot_wide(qeff, first_ref[h])
            qeff = out[:, :HD]
            local = local + out[:, HD:]
        qeff_ref[h, n * C : n * C + C, :] = qeff.astype(BF16)
        local_ref[h, n * C : n * C + C, :] = local


def y_index():
    return lax.rem(lax.div(lax.axis_index("ctx"), 2), 4)


def x_index():
    return lax.div(lax.axis_index("ctx"), 8)


def follow_sent(later, earlier):
    out = dot(later[:, :HD], earlier)
    return lanes(out[:, :HD], out[:, HD:] + later[:, HD:].astype(F32))


def row_kernel(m_ref, r1_ref, r2_ref, r3_ref, after, *refs):
    del after
    *total_refs, slots = refs
    y = y_index()
    for d, ref in enumerate((m_ref, r1_ref, r2_ref, r3_ref)):
        slots[jnp.bitwise_xor(y, d)] = ref[...]
    for h in range(OWN):
        m0, m1, m2, m3 = (slots[i, h] for i in range(4))
        total = follow(follow_sent(m3, m2), follow_sent(m1, m0)).astype(BF16)
        for ref in total_refs:
            ref[h] = total


def prefix_kernel(m_ref, r1_ref, r2_ref, r3_ref, early_ref, own_ref, other_ref, slots):
    core = core_index()
    y = y_index()
    for d, ref in enumerate((m_ref, r1_ref, r2_ref, r3_ref)):
        slots[jnp.bitwise_xor(y, d)] = ref[...]
    eye = (iota2((HD, 2 * HD), 0) == iota2((HD, 2 * HD), 1)).astype(F32)
    for h in range(OWN):
        m0, m1, m2 = (slots[i, h] for i in range(3))
        t01 = follow_sent(m1, m0)
        th, tl = split(t01)
        t012 = dot(m2[:, :HD], th) + dot(m2[:, :HD], tl)
        t012 = lanes(t012[:, :HD], t012[:, HD:] + m2[:, HD:].astype(F32))
        first = jnp.where(
            y == 0, eye, jnp.where(y == 1, m0.astype(F32), jnp.where(y == 2, t01, t012))
        )
        second = follow(early_ref[h], first)
        own_ref[h] = jnp.where(core == 0, first, second)
        other_ref[h] = jnp.where(core == 0, second, first)


def state_kernel(m_ref, r1_ref, r2_ref, r3_ref, own_ref, other_ref, keep_ref, send_ref, slots):
    x = x_index()
    for d, ref in enumerate((m_ref, r1_ref, r2_ref, r3_ref)):
        slots[jnp.bitwise_xor(x, d)] = ref[...]
    for h in range(OWN):
        m0, m1, m2 = (slots[i, h] for i in range(3))
        one = m0[:, HD:]
        two = dot(m1[:, :HD], one) + m1[:, HD:].astype(F32)
        three = dot_exact_left(m2[:, :HD], two) + m2[:, HD:].astype(F32)
        state = jnp.where(x == 1, one.astype(F32), jnp.where(x == 2, two, three))
        state = jnp.where(x > 0, state, 0.0)
        own, other = own_ref[h], other_ref[h]
        hi, lo = split(dot_sq(own[:, :HD], state) + own[:, HD:])
        keep_ref[h] = lanes(hi, lo)
        send_ref[h] = (dot_sq(other[:, :HD], state) + other[:, HD:]).astype(BF16)


def gated_rows(state, head, qeff_ref, local_ref, factor_ref):
    out = dot(qeff_ref[head], state)
    core_rows = local_ref[head] + out[:, :HD]
    if state.shape[1] > HD:
        core_rows = core_rows + out[:, HD:]
    mean = jnp.mean(core_rows * core_rows, axis=1, keepdims=True)
    return (core_rows * (1.0 / jnp.sqrt(mean + EPS)) * factor_ref[head]).astype(BF16)


def gather_rows(state_ref, first, qeff_ref, local_ref, factor_ref, gs, lhs):
    for h in range(OWN):
        gs[:, h * HD : h * HD + HD] = gated_rows(
            state_ref[h], first + h, qeff_ref, local_ref, factor_ref
        )
    me = lax.axis_index("tp")
    chunk = gs.shape[0] // TP
    for d in range(TP):
        start = pl.multiple_of(lax.rem(me + d, TP) * chunk, chunk)
        lhs[d * chunk : d * chunk + chunk, :] = gs[pl.ds(start, chunk), :]


def weight_rows(w_ref, first, s):
    return w_ref[pl.ds(pl.multiple_of(first * HD, OWN * HD), OWN * HD), s]


STEP = 512
ORDER_Y = (1, 2, 3)
ORDER_X = (1, 2, 3)


def own_kernel(state_ref, qeff_ref, local_ref, factor_ref, w_ref, acc_ref, gs, lhs):
    first = OWN * core_index()
    gather_rows(state_ref, first, qeff_ref, local_ref, factor_ref, gs, lhs)
    for j in range(w_ref.shape[1] // STEP):
        s = slice(j * STEP, j * STEP + STEP)
        acc_ref[:, s] = dot(lhs[...], weight_rows(w_ref, first, s))


def other_kernel(state_ref, acc_ref, qeff_ref, local_ref, factor_ref, w_ref, *refs):
    outs, (gs, lhs) = refs[:-2], refs[-2:]
    first = OWN * (1 - core_index())
    gather_rows(state_ref, first, qeff_ref, local_ref, factor_ref, gs, lhs)
    chunk = gs.shape[0] // TP
    for j in range(w_ref.shape[1] // STEP):
        s = slice(j * STEP, j * STEP + STEP)
        out = (acc_ref[:, s] + dot(lhs[...], weight_rows(w_ref, first, s))).astype(BF16)
        for d, ref in zip((0, 1, 2, 3, 5, 6, 7), outs):
            ref[:, s] = out[d * chunk : d * chunk + chunk]
        ref = outs[7 + j // 2]
        t = slice(j % 2 * STEP, j % 2 * STEP + STEP)
        ref[:, t] = out[4 * chunk : 5 * chunk]


def partial_kernel(a_ref, a3_ref, a4_ref, b_ref, b3_ref, b4_ref, ao_ref, bo_ref):
    half = a4_ref.shape[1]
    a = a_ref[...].astype(F32) + a3_ref[...].astype(F32)
    b = b_ref[...].astype(F32) + b3_ref[...].astype(F32)
    ao_ref[:, :half] = (a[:, :half] + a4_ref[...].astype(F32)).astype(BF16)
    ao_ref[:, half:] = a[:, half:].astype(BF16)
    bo_ref[:, :half] = b[:, :half].astype(BF16)
    bo_ref[:, half:] = (b[:, half:] + b4_ref[...].astype(F32)).astype(BF16)


def sum_kernel(*refs):
    total = refs[0][...].astype(F32)
    for ref in refs[1:-1]:
        total = total + ref[...].astype(F32)
    refs[-1][...] = total.astype(BF16)


def call(kernel, outs, args, scratch=(), hbm=(), flops=10**8, moved=2**20, vmem_mib=32):
    vmem = pl.BlockSpec(memory_space=pltpu.VMEM)
    stay = pl.BlockSpec(memory_space=pltpu.HBM)
    loose = pl.BlockSpec(memory_space=pl.ANY)
    specs = [{"hbm": stay, "any": loose}.get(dict(hbm).get(i), vmem) for i in range(len(args))]
    return pl.pallas_call(
        kernel,
        out_shape=[jax.ShapeDtypeStruct(s, t) for s, t in outs],
        in_specs=specs,
        out_specs=[vmem] * len(outs),
        scratch_shapes=list(scratch),
        compiler_params=pltpu.CompilerParams(vmem_limit_bytes=vmem_mib * 2**20),
        cost_estimate=pl.CostEstimate(flops=flops, bytes_accessed=moved, transcendentals=0),
    )(*args)


def on_device(q, k, v, ld, wr, gate, gain, w):
    tokens = q.shape[0]
    n_ctx = lax.axis_size("ctx")

    def swap(a):
        return lax.ppermute(a, "ctx", [(i, i ^ 1) for i in range(n_ctx)])

    def across_y(a, m):
        pairs = [(i, (i // 8 * 4 + (i // 2 % 4 ^ m)) * 2 + i % 2) for i in range(n_ctx)]
        return lax.ppermute(a, "ctx", pairs)

    def across_x(a, m):
        return lax.ppermute(a, "ctx", [(i, (i // 8 ^ m) * 8 + i % 8) for i in range(n_ctx)])

    def along_z(a, d):
        return lax.ppermute(a, "tp", [(i, (i + d) % TP) for i in range(TP)])

    pair = (OWN, HD, 2 * HD)
    wu, vec, vect, first, keep, send = call(
        maps_kernel,
        [
            ((NP, 2 * C, 2 * HD), BF16),
            ((8 * NP, C), F32),
            ((C, 8 * NP), F32),
            ((HEADS, HD, 2 * HD), F32),
            (pair, F32),
            (pair, BF16),
        ],
        tuple(pltpu.with_memory_space_constraint(a, pltpu.HBM) for a in (k, v, ld, wr)),
        [
            pltpu.VMEM(k.shape, BF16),
            pltpu.VMEM(v.shape, BF16),
            pltpu.VMEM(ld.shape, F32),
            pltpu.VMEM(wr.shape, F32),
            pltpu.VMEM((SUB * NP, C), F32),
            pltpu.VMEM((SUB * NP, C), F32),
            pltpu.SemaphoreType.DMA((4,)),
        ],
        hbm={0: "hbm", 1: "hbm", 2: "hbm", 3: "hbm"},
        flops=10**9,
        vmem_mib=32,
    )
    *totals, early = call(pair_kernel, [(pair, BF16)] * 3 + [(pair, F32)], (keep, swap(send)))
    total = totals[0]
    around = [across_y(totals[ORDER_Y.index(m)], m) for m in (1, 2, 3)]
    qeff, local, factor = call(
        reads_kernel,
        [((HEADS, tokens, HD), BF16)] + [((HEADS, tokens, HD), F32)] * 2,
        (q, k, wu, vec, vect, first, gate, gain.reshape(1, HD)),
        flops=10**9,
    )
    row_totals = call(
        row_kernel,
        [(pair, BF16)] * 3,
        (total, *around, local),
        [pltpu.VMEM((4, *pair), BF16)],
        hbm={4: "any"},
    )
    own, other = call(
        prefix_kernel,
        [(pair, F32)] * 2,
        (total, *around, early),
        [pltpu.VMEM((4, *pair), BF16)],
    )
    rows_around = [across_x(row_totals[ORDER_X.index(m)], m) for m in (1, 2, 3)]
    own_state, send_state = call(
        state_kernel,
        [(pair, BF16), ((OWN, HD, HD), BF16)],
        (row_totals[0], *rows_around, own, other),
        [pltpu.VMEM((4, *pair), BF16)],
    )
    other_state = swap(send_state)
    rows_scratch = [pltpu.VMEM((tokens, OWN * HD), BF16)] * 2
    width = w.shape[1]
    (acc,) = call(
        own_kernel,
        [((tokens, width), F32)],
        (own_state, qeff, local, factor, w),
        rows_scratch,
        flops=10**9,
    )
    rows_here = tokens // TP
    block = ((rows_here, width), BF16)
    p0, p1, p2, p3, p5, p6, p7, p4a, p4b = call(
        other_kernel,
        [block] * 7 + [((rows_here, width // 2), BF16)] * 2,
        (other_state, acc, qeff, local, factor, w),
        rows_scratch,
        flops=10**9,
    )
    a3, b3 = along_z(p3, 1), along_z(p5, -1)
    a4, b4 = along_z(p4a, 2), along_z(p4b, -2)
    a1, b1 = along_z(p1, 1), along_z(p7, -1)
    pa, pb = call(partial_kernel, [block] * 2, (p2, a3, a4, p6, b3, b4))
    a2, b2 = along_z(pa, 2), along_z(pb, -2)
    return call(sum_kernel, [block], (p0, a1, b1, a2, b2))[0]


def solution(mesh):
    in_specs = (
        P("ctx", "tp"),
        P("ctx", "tp"),
        P("ctx", "tp"),
        P("tp", "ctx"),
        P("tp", "ctx"),
        P("ctx", "tp"),
        P(),
        P("tp", None),
    )
    return jax.shard_map(
        on_device, mesh=mesh, in_specs=in_specs, out_specs=P(("ctx", "tp"), None), check_vma=False
    )
```
